32 devices in a mesh: tok: 8 (over z, x), wid: 4 (over y, core).
Axes of the slice: x: 2, y: 2, z: 4, core: 2. Of those that a mesh axis runs over, the one named last changes fastest.
Arguments:
- acts: bfloat16 [4096, 4096], P('tok', 'wid'), may hold values from -6 to 6
- grads: bfloat16 [4096, 11008], P('tok', 'wid'), may hold values from -6 to 6
- lengths: int32 [8], replicated, may hold values from 1 to 512, 3072 in all
Outputs:
- kernel_tiles: float32 [4096, 5, 512], P('tok', None, 'wid')
The draws below stay inside these ranges and needn't reach their ends.
Inputs may be any that keep to these rules, and one draw needn't show every extreme that they name: One block has all 512 slots live; the lengths sum to 3072.
All inputs are finite; a program needn't handle non-finite values.
Results may differ from the reference program's by a relative error of at most 0.00075.
Values may be sent and summed in bfloat16 or wider, within the bound.
No kernel may reach another device: no remote copies, remote signals or barrier semaphores. Data moves between devices by JAX's collectives and lax.ppermute only.
A program may use at most 128 MiB of HBM per device.

```python
import math
import jax
import jax.numpy as jnp
import numpy as np
from jax import lax

D = 4096
FF = 11008
TOK_DEV = 512
REACH = 2
TOKENS = 4096
N_TOK = 8


def levels(stream_key, shape, pieces, least, largest):
    def one(axis_at, shards_of):
        draws = jax.random.uniform(jax.random.fold_in(jax.random.fold_in(stream_key, 6), axis_at), (shards_of,), jnp.float32, least / len(pieces), largest / len(pieces))
        return jnp.repeat(jnp.exp(draws), shape[axis_at] // shards_of).reshape((-1,) + (1,) * (len(shape) - axis_at - 1))

    loudness = one(*pieces[0])
    for cut in pieces[1:]:
        loudness = loudness * one(*cut)
    return loudness


def split_up(number_of, total, bound, slope):
    loads = [(1 << 20) // math.isqrt(grade ** slope) + 1 for grade in range(2, number_of + 1)]
    rest, counts = total - bound - (number_of - 1), [1] * (number_of - 1)
    while rest > 0:
        candidates = [i for i in range(number_of - 1) if counts[i] < bound]
        mass, remaining = sum([loads[i] for i in candidates]), rest
        for i in candidates:
            addition = min(bound - counts[i], max(1, remaining * loads[i] // mass), rest)
            counts[i] = counts[i] + addition
            rest = rest - addition
    return np.array([bound] + counts)


def uneven(stream_key, number_of, total, limit, skew):
    if number_of == 2:
        one = jax.random.randint(stream_key, (), max(1, total - limit), min(limit, total - 1) + 1)
        return jnp.stack([one, total - one])
    sizes = jnp.asarray(split_up(number_of, total, limit, skew), jnp.int32)
    twos = (number_of - 1) // 2
    donor, taker = sizes[1:1 + 2 * twos:2], sizes[2:2 + 2 * twos:2]
    slack = jnp.minimum(donor - 1, limit - taker)
    moved = jax.random.randint(jax.random.fold_in(stream_key, 1), (twos,), 0, 1 << 20) % (slack + 1)
    sizes = sizes.at[1:1 + 2 * twos:2].set(donor - moved).at[2:2 + 2 * twos:2].set(taker + moved)
    return sizes[jax.random.permutation(jax.random.fold_in(stream_key, 2), number_of)]


def gaussian(rng, shape, width, limit, cuts=(), kind=jnp.bfloat16):
    gain = levels(rng, shape, cuts, -0.22, 0.18) if cuts else 1.0
    values = jax.random.normal(rng, shape, jnp.float32) * width * gain
    return jnp.minimum(jnp.maximum(values, -limit), limit).astype(kind)


def setup_inputs(seed: int = 0) -> dict:
    seeds = jax.random.split(jax.random.key(seed), 4)
    acts = gaussian(seeds[0], (TOKENS, D), 1.0, 6.0, ((0, 8), (1, 4)))
    grads = gaussian(seeds[1], (TOKENS, FF), 1.0, 6.0, ((0, 8), (1, 4)))
    lengths = uneven(seeds[2], N_TOK, 3 * TOK_DEV * N_TOK // 4, TOK_DEV, 2).astype(jnp.int32)
    return dict(acts=acts, grads=grads, lengths=lengths)


def reference(acts, grads, lengths):
    slots = jnp.arange(TOK_DEV, dtype=jnp.int32)
    live = (slots[None, :] < lengths[:, None]).astype(jnp.bfloat16)
    masked_acts = acts.reshape(N_TOK, TOK_DEV, D) * live[:, :, None]
    masked_grads = grads.reshape(N_TOK, TOK_DEV, FF) * live[:, :, None]

    def one_block(block):
        own_acts = masked_acts[block]
        own_grads = masked_grads[block]
        tiles = []
        for offset in range(2 * REACH + 1):
            partner = ((block + offset - REACH) % N_TOK).astype(jnp.int32)
            act_gram = jnp.dot(own_acts, masked_acts[partner].T, preferred_element_type=jnp.float32)
            grad_gram = jnp.dot(own_grads, masked_grads[partner].T, preferred_element_type=jnp.float32)
            tiles.append(act_gram / jnp.sqrt(jnp.float32(D)) * (grad_gram / jnp.sqrt(jnp.float32(FF))))
        return jnp.stack(tiles, axis=1)
    result = lax.map(one_block, jnp.arange(N_TOK, dtype=jnp.int32))
    return result.reshape(N_TOK * TOK_DEV, 2 * REACH + 1, TOK_DEV)
```

```python
import math

import jax
import jax.numpy as jnp
from jax import lax
from jax.experimental import pallas as pl
from jax.experimental.pallas import tpu as pltpu
from jax.sharding import PartitionSpec as P

D = 4096
FF = 11008
WID = 4
UNIT = 128
SUB = UNIT // WID


def gram(left, right):
    return lax.dot_general(left, right, (((1,), (1,)), ((), ())), preferred_element_type=jnp.float32)


def step_blocks(step, units):
    fresh = [(step, b) for b in range(step + 1)] + [(a, step) for a in range(step)]
    return (
        [("rt", a, step) for a in range(units)]
        + [("tt", b, a) for a, b in fresh]
        + [("tj", a, b) for a, b in fresh]
        + [("rj", step, b) for b in range(units)]
    )


def partial_kernel(names, units, place_ref, *refs):
    own, ring, other, (keep, send) = refs[:units], refs[units : 2 * units], refs[2 * units : -2], refs[-2:]
    even = place_ref[0] == 0
    core = place_ref[1]
    side = place_ref[2]
    spot = {name: i for i, name in enumerate(names)}

    def put(name, block):
        at = pl.ds(spot[name] * SUB, SUB)
        for quarter in range(WID):
            rows = block[quarter * SUB : (quarter + 1) * SUB]
            there = jnp.abs(side - quarter // 2)

            @pl.when(core == quarter % 2)
            def _():
                keep[there, at, :] = rows

            @pl.when(core != quarter % 2)
            def _():
                send[there, at, :] = rows

    for kind, a, b in names:
        if kind == "rj":
            block = gram(ring[a][...], own[b][...])
            put((kind, a, b), block)
            put(("rt", b, a), block.T)
        elif kind == "tj":
            chosen = jnp.where(even, ring[a][...], own[a][...])
            block = gram(chosen, other[b][...])
            put((kind, a, b), block)
            put(("tt", b, a), block.T)
        elif kind == "s":
            put((kind, a, b), gram(own[a][...], own[b][...]))


def partials(names, place, own, ring, other):
    units = len(own)
    shape = jax.ShapeDtypeStruct((2, len(names) * SUB, UNIT), jnp.float32)
    return pl.pallas_call(
        lambda *refs: partial_kernel(names, units, *refs),
        out_shape=(shape, shape),
        in_specs=[pl.BlockSpec(memory_space=pltpu.SMEM)] + [pl.BlockSpec(memory_space=pltpu.VMEM)] * (len(own) + len(ring) + len(other)),
        out_specs=(pl.BlockSpec(memory_space=pltpu.VMEM),) * 2,
        compiler_params=pltpu.CompilerParams(vmem_limit_bytes=40 << 20),
    )(place, *own, *ring, *other)


def wid_total(keep, send):
    arrived = lax.ppermute(send, "wid", [(w, w ^ 1) for w in range(WID)])
    across = lax.ppermute(keep[1] + arrived[1], "wid", [(w, w ^ 2) for w in range(WID)])
    return keep[0] + arrived[0] + across


def final_kernel(units, pieces, place_ref, lengths_ref, *refs):
    out = refs[-1]
    even = place_ref[0] == 0
    width = place_ref[3]
    token = place_ref[4]
    total = lengths_ref.shape[0]
    here = lengths_ref[token]
    for offset in range(5):
        there = lengths_ref[lax.rem(token + offset + total - 2, total)]
        for b in range(units):
            def piece(source):
                parts = []
                for a in range(units):
                    which, at = pieces[(source, a, b)]
                    parts.append(refs[which][at * SUB : (at + 1) * SUB, :])
                return jnp.concatenate(parts, axis=0)

            if offset == 1:
                tile = jnp.where(even, piece("ztt"), piece("tt"))
            else:
                tile = piece(("zrt", None, "s", "xtj", "rj")[offset])
            tile = tile.T
            columns = width * UNIT + lax.broadcasted_iota(jnp.int32, (SUB, UNIT), 1)
            for quarter in range(WID):
                first = quarter * UNIT + b * SUB
                rows = first + lax.broadcasted_iota(jnp.int32, (SUB, UNIT), 0)
                live = (rows < here) & (columns < there)
                out[first : first + SUB, offset, :] = jnp.where(live, tile[quarter * SUB : (quarter + 1) * SUB], 0.0)


def shards(acts, grads, lengths):
    rows = acts.shape[0]
    units = rows // UNIT
    length = lax.axis_size("tok")
    token = lax.axis_index("tok")
    width = lax.axis_index("wid")
    place = jnp.stack([token % 2, width % 2, width // 2, width, token]).astype(jnp.int32)
    swap = [(i, i ^ 1) for i in range(length)]
    down = [(i, (i - 2) % length) for i in range(length)]
    up = [(i, (i + 2) % length) for i in range(length)]

    def cut(x):
        x = x.reshape(WID, units, SUB, x.shape[1])
        return [x[:, c].reshape(UNIT, x.shape[3]) for c in range(units)]

    own_a = jnp.concatenate(cut(acts), axis=0)
    ring_a = lax.ppermute(own_a, "tok", down)
    other_a = lax.ppermute(own_a, "tok", swap)
    own_g = cut(grads)
    ring_g, other_g = [], []
    for c in range(units):
        chunk = own_g[c]
        if c >= 1:
            held = (ring_a, other_a) if c == 1 else (ring_g[c - 2], other_g[c - 2])
            chunk, first, second = lax.optimization_barrier((chunk, *held))
            if c == 1:
                ring_a, other_a = first, second
            else:
                ring_g[c - 2], other_g[c - 2] = first, second
        ring_g.append(lax.ppermute(chunk, "tok", down))
        other_g.append(lax.ppermute(chunk, "tok", swap))

    scale_a = 1.0 / jnp.sqrt(jnp.float32(D))
    scale_g = 1.0 / jnp.sqrt(jnp.float32(FF))
    pick = lambda x: [x[c * UNIT : (c + 1) * UNIT] for c in range(units)]

    self_names = [("s", a, b) for a in range(units) for b in range(units)]
    keep_a, send_a = partials(self_names, place, pick(own_a), [], [])
    keep_g, send_g = partials(self_names, place, own_g, [], [])
    both = wid_total(jnp.concatenate([keep_a, keep_g], axis=1), jnp.concatenate([send_a, send_g], axis=1))
    half = both.shape[0] // 2
    self_tile = (both[:half] * scale_a) * (both[half:] * scale_g)

    steps = [step_blocks(c, units) for c in range(units)]
    names = sum(steps, [])
    act_total = wid_total(*partials(names, place, pick(own_a), pick(ring_a), pick(other_a)))

    arrays, pieces = [self_tile], {("s", a, b): (0, i) for i, (_, a, b) in enumerate(self_names)}
    start = 0
    for c in range(units):
        size = len(steps[c])
        pad = lambda x: x[: c + 1] + [x[0]] * (units - c - 1)
        grad_total = wid_total(*partials(steps[c], place, own_g, pad(ring_g), pad(other_g)))
        tile = (act_total[start * SUB : (start + size) * SUB] * scale_a) * (grad_total * scale_g)
        start += size
        n_z, n_x = units + 2 * c + 1, 2 * c + 1
        arrays.append(tile)
        arrays.append(lax.ppermute(tile[: n_z * SUB], "tok", up))
        arrays.append(lax.ppermute(tile[n_z * SUB : (n_z + n_x) * SUB], "tok", swap))
        for i, (kind, a, b) in enumerate(steps[c]):
            if kind in ("rj", "tt"):
                pieces[(kind, a, b)] = (len(arrays) - 3, i)
            if kind in ("rt", "tt"):
                pieces[("z" + kind, a, b)] = (len(arrays) - 2, i)
            if kind == "tj":
                pieces[("xtj", a, b)] = (len(arrays) - 1, i - n_z)

    return pl.pallas_call(
        lambda *refs: final_kernel(units, pieces, *refs),
        out_shape=jax.ShapeDtypeStruct((rows, 5, UNIT), jnp.float32),
        in_specs=[pl.BlockSpec(memory_space=pltpu.SMEM)] * 2 + [pl.BlockSpec(memory_space=pltpu.VMEM)] * len(arrays),
        out_specs=pl.BlockSpec(memory_space=pltpu.VMEM),
        compiler_params=pltpu.CompilerParams(vmem_limit_bytes=32 << 20),
    )(place, lengths, *arrays)


def solution(mesh):
    return jax.shard_map(
        shards,
        mesh=mesh,
        in_specs=(P("tok", "wid"), P("tok", "wid"), P()),
        out_specs=P("tok", None, "wid"),
        check_vma=False,
    )
```

```python
import jax
import jax.numpy as jnp
from jax import lax
from jax.experimental import pallas as pl
from jax.experimental.pallas import tpu as pltpu
from jax.sharding import PartitionSpec as P

D = 4096
FF = 11008
WID = 4
UNIT = 128
SUB = UNIT // WID
VMEM_LIMIT = 24 << 20
SMEM = pl.BlockSpec(memory_space=pltpu.SMEM)
VMEM = pl.BlockSpec(memory_space=pltpu.VMEM)


def call(kernel, outs, *args, scalars=0):
    return pl.pallas_call(
        kernel,
        out_shape=outs,
        in_specs=[SMEM] * scalars + [VMEM] * (len(args) - scalars),
        out_specs=jax.tree.map(lambda _: VMEM, outs),
        cost_estimate=pl.CostEstimate(flops=0, bytes_accessed=0, transcendentals=0),
        compiler_params=pltpu.CompilerParams(vmem_limit_bytes=VMEM_LIMIT),
    )(*args)


def dot(left, right, dims):
    return lax.dot_general(left, right, (dims, ((), ())), preferred_element_type=jnp.float32)


def row_dot(left, right):
    return dot(left, right, ((1,), (1,)))


def put(place_ref, keep, send, at, quarters):
    core = place_ref[1] == 0
    side = place_ref[2] == 0
    rows = pl.ds(at, quarters[0].shape[0])
    kept = [jnp.where(core, quarters[2 * s], quarters[2 * s + 1]) for s in range(2)]
    sent = [jnp.where(core, quarters[2 * s + 1], quarters[2 * s]) for s in range(2)]
    for ref, pair in ((keep, kept), (send, sent)):
        ref[0, rows, :] = jnp.where(side, pair[0], pair[1])
        ref[1, rows, :] = jnp.where(side, pair[1], pair[0])


def split_rows(block):
    n = block.shape[0] // WID
    return [block[q * n : (q + 1) * n] for q in range(WID)]


def lanes(block, b):
    return block[:, b * UNIT : (b + 1) * UNIT]


def step_layout(step, units):
    fresh = [(step, b) for b in range(step + 1)] + [(a, step) for a in range(step)]
    at, spot = UNIT, {("rt", step): 0}
    for a, b in fresh:
        spot[("tt", b, a)] = at
        at += SUB
    n_ring = at
    for a, b in fresh:
        spot[("tj", a, b)] = at
        at += SUB
    n_swap = at
    for b in range(WID):
        spot[("rj", step, b)] = at
        at += SUB
    return spot, n_ring, n_swap, at


def put_ring(place_ref, keep, send, spot, base, step, block):
    columns = [lanes(block, b) for b in range(WID)]
    put(place_ref, keep, send, base + spot[("rt", step)], [c.T for c in columns])
    for b in range(WID):
        put(place_ref, keep, send, base + spot[("rj", step, b)], split_rows(columns[b]))


def put_third(place_ref, keep, send, spot, base, a, b, block):
    put(place_ref, keep, send, base + spot[("tj", a, b)], split_rows(block))
    put(place_ref, keep, send, base + spot[("tt", b, a)], split_rows(block.T))


def reorder_kernel(g_ref, *outs):
    units = len(outs)
    tokens = g_ref.shape[1]
    source = lax.broadcasted_iota(jnp.int32, (tokens, UNIT), 0)
    lane = lax.broadcasted_iota(jnp.int32, (tokens, UNIT), 1)
    for c, out in enumerate(outs):
        wanted = (lane // SUB) * UNIT + c * SUB + lane % SUB
        pick = jnp.where(source == wanted, 1.0, 0.0).astype(jnp.bfloat16)
        out[...] = dot(g_ref[...], pick, ((1,), (0,))).astype(jnp.bfloat16)


def self_kernel(place_ref, a_ref, g_ref, keep, send):
    acts = a_ref[...]
    grads = g_ref[...]
    for i, block in enumerate((row_dot(acts, acts), dot(grads.T, grads, ((1,), (0,))))):
        for b in range(WID):
            put(place_ref, keep, send, (i * WID + b) * UNIT, split_rows(lanes(block, b)))


def acts_kernel(layouts, place_ref, own_ref, ring_ref, other_ref, keep, send):
    units = len(layouts)
    even = place_ref[0] == 0

    def arrival(x):
        return jnp.concatenate([x[q * UNIT + c * SUB : q * UNIT + (c + 1) * SUB] for c in range(units) for q in range(WID)], axis=0)

    own, ring, other = own_ref[...], ring_ref[...], other_ref[...]
    chosen = arrival(jnp.where(even, ring, own))
    ring = arrival(ring)
    other = arrival(other)
    base = 0
    for c, (spot, _, _, size) in enumerate(layouts):
        put_ring(place_ref, keep, send, spot, base, c, row_dot(ring[c * UNIT : (c + 1) * UNIT], own))
        base += size
    for a in range(units):
        block = row_dot(chosen[a * UNIT : (a + 1) * UNIT], other)
        for b in range(units):
            step = max(a, b)
            base = sum(layouts[s][3] for s in range(step))
            put_third(place_ref, keep, send, layouts[step][0], base, a, b, lanes(block, b))


def grads_kernel(step, spot, place_ref, own_ref, *refs):
    n = step + 1
    mine, ring, other, (keep, send) = refs[:n], refs[n : 2 * n], refs[2 * n : 3 * n], refs[3 * n :]
    even = place_ref[0] == 0
    chosen = [jnp.where(even, ring[a][...], mine[a][...]) for a in range(n)]
    put_ring(place_ref, keep, send, spot, 0, step, dot(ring[step][...].T, own_ref[...], ((1,), (0,))))
    block = dot(chosen[step].T, jnp.concatenate([o[...] for o in other], axis=1), ((1,), (0,)))
    for b in range(n):
        put_third(place_ref, keep, send, spot, 0, step, b, lanes(block, b))
    if step:
        block = dot(other[step][...].T, jnp.concatenate(chosen[:step], axis=1), ((1,), (0,))).T
        for a in range(step):
            put_third(place_ref, keep, send, spot, 0, a, step, block[a * UNIT : (a + 1) * UNIT])


def final_kernel(layouts, place_ref, lengths_ref, self_ref, *refs):
    out = refs[-1]
    units = len(layouts)
    local, ring, swap = refs[:units], refs[units : 2 * units], refs[2 * units : 3 * units]
    even = place_ref[0] == 0
    width = place_ref[3]
    token = place_ref[4]
    total = lengths_ref.shape[0]
    here = lengths_ref[token]
    columns = width * UNIT + lax.broadcasted_iota(jnp.int32, (UNIT, UNIT), 1)
    line = lax.broadcasted_iota(jnp.int32, (UNIT, UNIT), 0)

    def block(refs, name, step, shift=0):
        spot = layouts[step][0][name] - shift
        size = UNIT if name[0] == "rt" else SUB
        return refs[step][spot : spot + size, :]

    def natural(offset, b, tile, there):
        live = (b * UNIT + line < here) & (columns < there)
        out[offset, b * UNIT : (b + 1) * UNIT, :] = jnp.where(live, tile.T, 0.0)

    def arrival(offset, c, tile, there):
        token_at = (line // SUB) * UNIT + c * SUB + line % SUB
        tile = jnp.where((token_at < here) & (columns < there), tile.T, 0.0)
        for q in range(WID):
            first = q * UNIT + c * SUB
            out[offset, first : first + SUB, :] = tile[q * SUB : (q + 1) * SUB]

    there = [lengths_ref[lax.rem(token + offset + total - 2, total)] for offset in range(5)]
    for c in range(units):
        arrival(0, c, block(ring, ("rt", c), c), there[0])
        tt = [[block(r, ("tt", a, c), max(a, c)) for a in range(units)] for r in (ring, local)]
        arrival(1, c, jnp.where(even, jnp.concatenate(tt[0], axis=0), jnp.concatenate(tt[1], axis=0)), there[1])
        tj = [block(swap, ("tj", a, c), max(a, c), layouts[max(a, c)][1]) for a in range(units)]
        arrival(3, c, jnp.concatenate(tj, axis=0), there[3])
    for b in range(WID):
        natural(2, b, self_ref[b * UNIT : (b + 1) * UNIT, :], there[2])
        natural(4, b, jnp.concatenate([block(local, ("rj", c, b), c) for c in range(units)], axis=0), there[4])


def shards(acts, grads, lengths):
    rows = acts.shape[0]
    units = rows // UNIT
    length = lax.axis_size("tok")
    token = lax.axis_index("tok")
    width = lax.axis_index("wid")
    place = jnp.stack([token % 2, width % 2, width // 2, width, token]).astype(jnp.int32)
    swap = [(i, i ^ 1) for i in range(length)]
    down = [(i, (i - 2) % length) for i in range(length)]
    up = [(i, (i + 2) % length) for i in range(length)]
    layouts = [step_layout(c, units) for c in range(units)]

    def floats(n):
        return (jax.ShapeDtypeStruct((2, n, UNIT), jnp.float32),) * 2

    def wid_total(keep, send):
        arrived = lax.ppermute(send, "wid", [(w, w ^ 1) for w in range(WID)])
        across = lax.ppermute(keep[1] + arrived[1], "wid", [(w, w ^ 2) for w in range(WID)])
        return keep[0], arrived[0], across

    def total(parts, start, stop):
        return parts[0][start:stop] + parts[1][start:stop] + parts[2][start:stop]

    scale_a = 1.0 / jnp.sqrt(jnp.float32(D))
    scale_g = 1.0 / jnp.sqrt(jnp.float32(FF))

    ring_a = lax.ppermute(acts, "tok", down)
    other_a = lax.ppermute(acts, "tok", swap)
    own_g = grads.T
    mine = call(reorder_kernel, (jax.ShapeDtypeStruct((grads.shape[1], UNIT), jnp.bfloat16),) * units, own_g)
    ring_g, other_g = [], []
    for c in range(units):
        chunk = mine[c]
        if c == 1:
            chunk, ring_a, other_a = lax.optimization_barrier((chunk, ring_a, other_a))
        elif c > 1:
            chunk, ring_g[c - 2], other_g[c - 2] = lax.optimization_barrier((chunk, ring_g[c - 2], other_g[c - 2]))
        ring_g.append(lax.ppermute(chunk, "tok", down))
        other_g.append(lax.ppermute(chunk, "tok", swap))

    parts = wid_total(*call(self_kernel, floats(2 * WID * UNIT), place, acts, own_g, scalars=1))
    half = WID * UNIT
    self_tile = (total(parts, 0, half) * scale_a) * (total(parts, half, 2 * half) * scale_g)

    everything = sum(size for _, _, _, size in layouts)
    act_parts = wid_total(
        *call(lambda *refs: acts_kernel(layouts, *refs), floats(everything), place, acts, ring_a, other_a, scalars=1)
    )

    local, from_ring, from_swap = [], [], []
    base = 0
    for c, (spot, n_ring, n_swap, size) in enumerate(layouts):
        parts = wid_total(
            *call(
                lambda *refs, c=c, spot=spot: grads_kernel(c, spot, *refs),
                floats(size), place, own_g, *mine[: c + 1], *ring_g[: c + 1], *other_g[: c + 1], scalars=1,
            )
        )
        tile = (total(act_parts, base, base + size) * scale_a) * (total(parts, 0, size) * scale_g)
        base += size
        local.append(tile)
        from_ring.append(lax.ppermute(tile[:n_ring], "tok", up))
        from_swap.append(lax.ppermute(tile[n_ring:n_swap], "tok", swap))

    out = call(
        lambda *refs: final_kernel(layouts, *refs),
        jax.ShapeDtypeStruct((5, rows, UNIT), jnp.float32),
        place, lengths, self_tile, *local, *from_ring, *from_swap, scalars=2,
    )
    return out.transpose(1, 0, 2)


def solution(mesh):
    return jax.shard_map(
        shards,
        mesh=mesh,
        in_specs=(P("tok", "wid"), P("tok", "wid"), P()),
        out_specs=P("tok", None, "wid"),
        check_vma=False,
    )
```

```python
import jax
import jax.numpy as jnp
from jax import lax
from jax.experimental import pallas as pl
from jax.experimental.pallas import tpu as pltpu
from jax.sharding import PartitionSpec as P

D = 4096
FF = 11008
WID = 4
UNIT = 128
SUB = UNIT // WID
VMEM_LIMIT = 24 << 20
SMEM = pl.BlockSpec(memory_space=pltpu.SMEM)
VMEM = pl.BlockSpec(memory_space=pltpu.VMEM)


def call(kernel, outs, *args, scalars=0):
    return pl.pallas_call(
        kernel,
        out_shape=outs,
        in_specs=[SMEM] * scalars + [VMEM] * (len(args) - scalars),
        out_specs=jax.tree.map(lambda _: VMEM, outs),
        cost_estimate=pl.CostEstimate(flops=0, bytes_accessed=0, transcendentals=0),
        compiler_params=pltpu.CompilerParams(vmem_limit_bytes=VMEM_LIMIT),
    )(*args)


def dot(left, right, dims):
    return lax.dot_general(left, right, (dims, ((), ())), preferred_element_type=jnp.float32)


def row_dot(left, right):
    return dot(left, right, ((1,), (1,)))


def put(place_ref, keep, send, at, quarters):
    core = place_ref[1] == 0
    side = place_ref[2] == 0
    rows = pl.ds(at, quarters[0].shape[0])
    kept = [jnp.where(core, quarters[2 * s], quarters[2 * s + 1]) for s in range(2)]
    sent = [jnp.where(core, quarters[2 * s + 1], quarters[2 * s]) for s in range(2)]
    for ref, pair in ((keep, kept), (send, sent)):
        ref[0, rows, :] = jnp.where(side, pair[0], pair[1])
        ref[1, rows, :] = jnp.where(side, pair[1], pair[0])


def split_rows(block):
    n = block.shape[0] // WID
    return [block[q * n : (q + 1) * n] for q in range(WID)]


def lanes(block, b):
    return block[:, b * UNIT : (b + 1) * UNIT]


def step_layout(step, units):
    fresh = [(step, b) for b in range(step + 1)] + [(a, step) for a in range(step)]
    at, spot = UNIT, {("rt", step): 0}
    for a, b in fresh:
        spot[("tt", b, a)] = at
        at += SUB
    n_ring = at
    for a, b in fresh:
        spot[("tj", a, b)] = at
        at += SUB
    n_swap = at
    for b in range(WID):
        spot[("rj", step, b)] = at
        at += SUB
    return spot, n_ring, n_swap, at


def put_ring(place_ref, keep, send, spot, base, step, block):
    columns = [lanes(block, b) for b in range(WID)]
    put(place_ref, keep, send, base + spot[("rt", step)], [c.T for c in columns])
    for b in range(WID):
        put(place_ref, keep, send, base + spot[("rj", step, b)], split_rows(columns[b]))


def put_third(place_ref, keep, send, spot, base, a, b, block):
    put(place_ref, keep, send, base + spot[("tj", a, b)], split_rows(block))
    put(place_ref, keep, send, base + spot[("tt", b, a)], split_rows(block.T))


def reorder_kernel(g_ref, *outs):
    units = len(outs)
    tokens = g_ref.shape[1]
    source = lax.broadcasted_iota(jnp.int32, (tokens, UNIT), 0)
    lane = lax.broadcasted_iota(jnp.int32, (tokens, UNIT), 1)
    for c, out in enumerate(outs):
        wanted = (lane // SUB) * UNIT + c * SUB + lane % SUB
        pick = jnp.where(source == wanted, 1.0, 0.0).astype(jnp.bfloat16)
        out[...] = dot(g_ref[...], pick, ((1,), (0,))).astype(jnp.bfloat16)


def self_kernel(place_ref, a_ref, g_ref, keep, send):
    acts = a_ref[...]
    grads = g_ref[...]
    for i, block in enumerate((row_dot(acts, acts), dot(grads.T, grads, ((1,), (0,))))):
        for b in range(WID):
            put(place_ref, keep, send, (i * WID + b) * UNIT, split_rows(lanes(block, b)))


def acts_kernel(layouts, place_ref, own_ref, ring_ref, other_ref, keep, send):
    units = len(layouts)
    even = place_ref[0] == 0

    def arrival(x):
        return jnp.concatenate([x[q * UNIT + c * SUB : q * UNIT + (c + 1) * SUB] for c in range(units) for q in range(WID)], axis=0)

    own, ring, other = own_ref[...], ring_ref[...], other_ref[...]
    chosen = arrival(jnp.where(even, ring, own))
    ring = arrival(ring)
    other = arrival(other)
    base = 0
    for c, (spot, _, _, size) in enumerate(layouts):
        put_ring(place_ref, keep, send, spot, base, c, row_dot(ring[c * UNIT : (c + 1) * UNIT], own))
        base += size
    for a in range(units):
        block = row_dot(chosen[a * UNIT : (a + 1) * UNIT], other)
        for b in range(units):
            step = max(a, b)
            base = sum(layouts[s][3] for s in range(step))
            put_third(place_ref, keep, send, layouts[step][0], base, a, b, lanes(block, b))


def grads_kernel(step, spot, place_ref, own_ref, *refs):
    n = step + 1
    mine, ring, other, (keep, send) = refs[:n], refs[n : 2 * n], refs[2 * n : 3 * n], refs[3 * n :]
    even = place_ref[0] == 0
    chosen = [jnp.where(even, ring[a][...], mine[a][...]) for a in range(n)]
    put_ring(place_ref, keep, send, spot, 0, step, dot(ring[step][...].T, own_ref[...], ((1,), (0,))))
    block = dot(chosen[step].T, jnp.concatenate([o[...] for o in other], axis=1), ((1,), (0,)))
    for b in range(n):
        put_third(place_ref, keep, send, spot, 0, step, b, lanes(block, b))
    if step:
        block = dot(other[step][...].T, jnp.concatenate(chosen[:step], axis=1), ((1,), (0,))).T
        for a in range(step):
            put_third(place_ref, keep, send, spot, 0, a, step, block[a * UNIT : (a + 1) * UNIT])


def final_kernel(layouts, place_ref, lengths_ref, self_ref, *refs):
    out = refs[-1]
    units = len(layouts)
    local, ring, swap = refs[:units], refs[units : 2 * units], refs[2 * units : 3 * units]
    even = place_ref[0] == 0
    width = place_ref[3]
    token = place_ref[4]
    total = lengths_ref.shape[0]
    here = lengths_ref[token]
    columns = width * UNIT + lax.broadcasted_iota(jnp.int32, (UNIT, UNIT), 1)
    line = lax.broadcasted_iota(jnp.int32, (UNIT, UNIT), 0)

    def block(refs, name, step, shift=0):
        spot = layouts[step][0][name] - shift
        size = UNIT if name[0] == "rt" else SUB
        return refs[step][spot : spot + size, :]

    def natural(offset, b, tile, there):
        live = (b * UNIT + line < here) & (columns < there)
        out[offset, b * UNIT : (b + 1) * UNIT, :] = jnp.where(live, tile.T, 0.0)

    def arrival(offset, c, tile, there):
        token_at = (line // SUB) * UNIT + c * SUB + line % SUB
        tile = jnp.where((token_at < here) & (columns < there), tile.T, 0.0)
        for q in range(WID):
            first = q * UNIT + c * SUB
            out[offset, first : first + SUB, :] = tile[q * SUB : (q + 1) * SUB]

    there = [lengths_ref[lax.rem(token + offset + total - 2, total)] for offset in range(5)]
    for c in range(units):
        arrival(0, c, block(ring, ("rt", c), c), there[0])
        tt = [[block(r, ("tt", a, c), max(a, c)) for a in range(units)] for r in (ring, local)]
        arrival(1, c, jnp.where(even, jnp.concatenate(tt[0], axis=0), jnp.concatenate(tt[1], axis=0)), there[1])
        tj = [block(swap, ("tj", a, c), max(a, c), layouts[max(a, c)][1]) for a in range(units)]
        arrival(3, c, jnp.concatenate(tj, axis=0), there[3])
    for b in range(WID):
        natural(2, b, self_ref[b * UNIT : (b + 1) * UNIT, :], there[2])
        natural(4, b, jnp.concatenate([block(local, ("rj", c, b), c) for c in range(units)], axis=0), there[4])


def shards(acts, grads, lengths):
    rows = acts.shape[0]
    units = rows // UNIT
    length = lax.axis_size("tok")
    token = lax.axis_index("tok")
    width = lax.axis_index("wid")
    place = jnp.stack([token % 2, width % 2, width // 2, width, token]).astype(jnp.int32)
    swap = [(i, i ^ 1) for i in range(length)]
    down = [(i, (i - 2) % length) for i in range(length)]
    up = [(i, (i + 2) % length) for i in range(length)]
    layouts = [step_layout(c, units) for c in range(units)]

    def floats(n):
        return (jax.ShapeDtypeStruct((2, n, UNIT), jnp.float32),) * 2

    scale_a = 1.0 / jnp.sqrt(jnp.float32(D))
    scale_g = 1.0 / jnp.sqrt(jnp.float32(FF))

    def tie(*arrays):
        return lax.optimization_barrier(arrays)

    def over_core(send):
        return lax.ppermute(send, "wid", [(w, w ^ 1) for w in range(WID)])

    def over_side(keep, arrived):
        return lax.ppermute(keep[1] + arrived[1], "wid", [(w, w ^ 2) for w in range(WID)])

    ring_a = lax.ppermute(acts, "tok", down)
    other_a = lax.ppermute(acts, "tok", swap)
    own_g = grads.T
    mine = list(call(reorder_kernel, (jax.ShapeDtypeStruct((grads.shape[1], UNIT), jnp.bfloat16),) * units, own_g))
    ring_g, other_g = [None] * units, [None] * units

    def start(chunk, *held):
        if held:
            chunk, *held = tie(chunk, *held)
        return lax.ppermute(chunk, "tok", down), lax.ppermute(chunk, "tok", swap), held

    ring_g[0], other_g[0], _ = start(mine[0])
    ring_g[1], other_g[1], (ring_a, other_a) = start(mine[1], ring_a, other_a)
    ring_g[2], other_g[2], (ring_g[0], other_g[0]) = start(mine[2], ring_g[0], other_g[0])

    alive = jnp.max(lengths) > 0

    def exchange(kernel, n, *args):
        def summed(*args):
            keep, send = call(kernel, floats(n), *args, scalars=1)
            arrived = over_core(send)
            return keep[0] + arrived[0] + over_side(keep, arrived)

        return lax.cond(alive, summed, lambda *args: jnp.zeros((n, UNIT), jnp.float32), *args)

    self_sum = exchange(self_kernel, 2 * WID * UNIT, place, acts, own_g)

    everything = sum(size for _, _, _, size in layouts)
    act_sum = exchange(lambda *refs: acts_kernel(layouts, *refs), everything, place, acts, ring_a, other_a)
    half = WID * UNIT
    self_tile = (self_sum[:half] * scale_a) * (self_sum[half:] * scale_g)

    last = units - 1
    cut = mine[last].shape[0] // 2
    piece = [mine[last][:cut], mine[last][cut:]]
    first_ring, first_other, (ring_g[1], other_g[1]) = start(piece[0], ring_g[1], other_g[1])
    second_ring, second_other, (ring_g[2], other_g[2]) = start(piece[1], ring_g[2], other_g[2])
    local = []
    base = 0
    for c, (spot, n_ring, n_swap, size) in enumerate(layouts):
        if c == last:
            ring_g[c] = jnp.concatenate([first_ring, second_ring], axis=0)
            other_g[c] = jnp.concatenate([first_other, second_other], axis=0)
        grad_sum = exchange(
            lambda *refs, c=c, spot=spot: grads_kernel(c, spot, *refs),
            size, place, own_g, *mine[: c + 1], *ring_g[: c + 1], *other_g[: c + 1],
        )
        local.append((act_sum[base : base + size] * scale_a) * (grad_sum * scale_g))
        base += size

    def back(tiles, steps):
        ring = jnp.concatenate([tiles[c][: layouts[c][1]] for c in steps], axis=0)
        swapped = jnp.concatenate([tiles[c][layouts[c][1] : layouts[c][2]] for c in steps], axis=0)
        return lax.ppermute(ring, "tok", up), lax.ppermute(swapped, "tok", swap)

    early = back(local, range(units - 1))
    late = back(local, [units - 1])

    def apart(joined, widths):
        ends = [sum(widths[:i]) for i in range(len(widths) + 1)]
        return [joined[a:b] for a, b in zip(ends, ends[1:])]

    from_ring = apart(early[0], [n for _, n, _, _ in layouts[:-1]]) + [late[0]]
    from_swap = apart(early[1], [m - n for _, n, m, _ in layouts[:-1]]) + [late[1]]

    out = call(
        lambda *refs: final_kernel(layouts, *refs),
        jax.ShapeDtypeStruct((5, rows, UNIT), jnp.float32),
        place, lengths, self_tile, *local, *from_ring, *from_swap, scalars=2,
    )
    return out.transpose(1, 0, 2)


def solution(mesh):
    return jax.shard_map(
        shards,
        mesh=mesh,
        in_specs=(P("tok", "wid"), P("tok", "wid"), P()),
        out_specs=P("tok", None, "wid"),
        check_vma=False,
    )
```

```python
import math

import jax
import jax.numpy as jnp
from jax import lax
from jax.experimental import pallas as pl
from jax.experimental.pallas import tpu as pltpu
from jax.sharding import PartitionSpec as P

D = 4096
FF = 11008
WID = 4
UNIT = 128
SUB = UNIT // WID
VMEM_LIMIT = 24 << 20
PIECES = ['A', '0', 'kS', '1', 'kA', '2', '3', 'k0', 'k1', 'k2', 'k3']
GATES = {'R1': ['RA'], 'O1': ['OA'], 'R2': ['RA'], 'O2': ['OA'], 'R3': ['R0'], 'O3': ['O0'], 'KA': ['SS'], 'K0': ['SA', 'R1', 'O1'], 'K1': ['SA'], 'K2': ['S1'], 'K3': ['S0', 'S1'], 'SA': [], 'S0': ['SA'], 'S1': [], 'S2': [], 'S3': ['S0', 'S1'], 'G0': [], 'G1': []}
PLAIN = []
GROUPS = [[0, 1, 2], [3]]
SMEM = pl.BlockSpec(memory_space=pltpu.SMEM)
VMEM = pl.BlockSpec(memory_space=pltpu.VMEM)


def call(kernel, outs, *args, scalars=0):
    return pl.pallas_call(
        kernel,
        out_shape=outs,
        in_specs=[SMEM] * scalars + [VMEM] * (len(args) - scalars),
        out_specs=jax.tree.map(lambda _: VMEM, outs),
        cost_estimate=pl.CostEstimate(flops=2000000000, bytes_accessed=2000000, transcendentals=0),
        compiler_params=pltpu.CompilerParams(vmem_limit_bytes=VMEM_LIMIT),
    )(*args)


def dot(left, right, dims):
    return lax.dot_general(left, right, (dims, ((), ())), preferred_element_type=jnp.float32)


def row_dot(left, right):
    return dot(left, right, ((1,), (1,)))


def put(place_ref, keep, send, at, quarters):
    core = place_ref[1] == 0
    side = place_ref[2] == 0
    rows = pl.ds(at, quarters[0].shape[0])
    kept = [jnp.where(core, quarters[2 * s], quarters[2 * s + 1]) for s in range(2)]
    sent = [jnp.where(core, quarters[2 * s + 1], quarters[2 * s]) for s in range(2)]
    for ref, pair in ((keep, kept), (send, sent)):
        ref[0, rows, :] = jnp.where(side, pair[0], pair[1])
        ref[1, rows, :] = jnp.where(side, pair[1], pair[0])


def split_rows(block):
    n = block.shape[0] // WID
    return [block[q * n : (q + 1) * n] for q in range(WID)]


def lanes(block, b):
    return block[:, b * UNIT : (b + 1) * UNIT]


def step_layout(step, units):
    fresh = [(step, b) for b in range(step + 1)] + [(a, step) for a in range(step)]
    at, spot = UNIT, {("rt", step): 0}
    for a, b in fresh:
        spot[("tt", b, a)] = at
        at += SUB
    n_ring = at
    for a, b in fresh:
        spot[("tj", a, b)] = at
        at += SUB
    n_swap = at
    for b in range(WID):
        spot[("rj", step, b)] = at
        at += SUB
    return spot, n_ring, n_swap, at


def put_ring(place_ref, keep, send, spot, base, step, block):
    columns = [lanes(block, b) for b in range(WID)]
    put(place_ref, keep, send, base + spot[("rt", step)], [c.T for c in columns])
    for b in range(WID):
        put(place_ref, keep, send, base + spot[("rj", step, b)], split_rows(columns[b]))


def put_third(place_ref, keep, send, spot, base, a, b, block):
    put(place_ref, keep, send, base + spot[("tj", a, b)], split_rows(block))
    put(place_ref, keep, send, base + spot[("tt", b, a)], split_rows(block.T))


def reorder_kernel(g_ref, *outs):
    units = len(outs)
    tokens = g_ref.shape[1]
    source = lax.broadcasted_iota(jnp.int32, (tokens, UNIT), 0)
    lane = lax.broadcasted_iota(jnp.int32, (tokens, UNIT), 1)
    for c, out in enumerate(outs):
        wanted = (lane // SUB) * UNIT + c * SUB + lane % SUB
        pick = jnp.where(source == wanted, 1.0, 0.0).astype(jnp.bfloat16)
        out[...] = dot(g_ref[...], pick, ((1,), (0,))).astype(jnp.bfloat16)


def self_kernel(place_ref, a_ref, g_ref, keep, send):
    acts = a_ref[...]
    grads = g_ref[...]
    for i, block in enumerate((row_dot(acts, acts), dot(grads.T, grads, ((1,), (0,))))):
        for b in range(WID):
            put(place_ref, keep, send, (i * WID + b) * UNIT, split_rows(lanes(block, b)))


def acts_kernel(layouts, place_ref, own_ref, ring_ref, other_ref, keep, send):
    units = len(layouts)
    even = place_ref[0] == 0

    def arrival(x):
        return jnp.concatenate([x[q * UNIT + c * SUB : q * UNIT + (c + 1) * SUB] for c in range(units) for q in range(WID)], axis=0)

    own, ring, other = own_ref[...], ring_ref[...], other_ref[...]
    chosen = arrival(jnp.where(even, ring, own))
    ring = arrival(ring)
    other = arrival(other)
    base = 0
    for c, (spot, _, _, size) in enumerate(layouts):
        put_ring(place_ref, keep, send, spot, base, c, row_dot(ring[c * UNIT : (c + 1) * UNIT], own))
        base += size
    for a in range(units):
        block = row_dot(chosen[a * UNIT : (a + 1) * UNIT], other)
        for b in range(units):
            step = max(a, b)
            base = sum(layouts[s][3] for s in range(step))
            put_third(place_ref, keep, send, layouts[step][0], base, a, b, lanes(block, b))


def grads_kernel(step, spot, place_ref, own_ref, *refs):
    n = step + 1
    mine, ring, other, (keep, send) = refs[:n], refs[n : 2 * n], refs[2 * n : 3 * n], refs[3 * n :]
    even = place_ref[0] == 0
    chosen = [jnp.where(even, ring[a][...], mine[a][...]) for a in range(n)]
    put_ring(place_ref, keep, send, spot, 0, step, dot(ring[step][...].T, own_ref[...], ((1,), (0,))))
    block = dot(chosen[step].T, jnp.concatenate([o[...] for o in other], axis=1), ((1,), (0,)))
    for b in range(n):
        put_third(place_ref, keep, send, spot, 0, step, b, lanes(block, b))
    if step:
        block = dot(other[step][...].T, jnp.concatenate(chosen[:step], axis=1), ((1,), (0,))).T
        for a in range(step):
            put_third(place_ref, keep, send, spot, 0, a, step, block[a * UNIT : (a + 1) * UNIT])


def product(acts, grads, act_at, grad_at, rows):
    act_sum = acts[0][act_at : act_at + rows, :] + acts[1][act_at : act_at + rows, :]
    grad_sum = grads[0][grad_at : grad_at + rows, :] + grads[1][grad_at : grad_at + rows, :]
    return (act_sum * (1.0 / math.sqrt(D))) * (grad_sum * (1.0 / math.sqrt(FF)))


def return_kernel(layouts, steps, *refs):
    acts, (ring, swap) = refs[:2], refs[-2:]
    ring_at = swap_at = 0
    for i, c in enumerate(steps):
        grads = refs[2 + 2 * i : 4 + 2 * i]
        _, n_ring, n_swap, _ = layouts[c]
        base = sum(layouts[s][3] for s in range(c))
        ring[ring_at : ring_at + n_ring, :] = product(acts, grads, base, 0, n_ring)
        swap[swap_at : swap_at + n_swap - n_ring, :] = product(acts, grads, base + n_ring, n_ring, n_swap - n_ring)
        ring_at += n_ring
        swap_at += n_swap - n_ring


def final_kernel(layouts, groups, place_ref, lengths_ref, *refs):
    units = len(layouts)
    selves, acts, out = refs[:2], refs[2:4], refs[-1]
    grads = [refs[4 + 2 * c : 6 + 2 * c] for c in range(units)]
    returned = {}
    for i, steps in enumerate(groups):
        ring, swap = refs[4 + 2 * units + 2 * i : 6 + 2 * units + 2 * i]
        ring_at = swap_at = 0
        for c in steps:
            _, n_ring, n_swap, _ = layouts[c]
            returned[c] = ring, ring_at, swap, swap_at - n_ring
            ring_at += n_ring
            swap_at += n_swap - n_ring
    even = place_ref[0] == 0
    width = place_ref[3]
    token = place_ref[4]
    total = lengths_ref.shape[0]
    here = lengths_ref[token]
    columns = width * UNIT + lax.broadcasted_iota(jnp.int32, (UNIT, UNIT), 1)
    line = lax.broadcasted_iota(jnp.int32, (UNIT, UNIT), 0)

    def block(where, name, step):
        spot = layouts[step][0][name]
        size = UNIT if name[0] == "rt" else SUB
        if where == "local":
            base = sum(layouts[s][3] for s in range(step))
            return product(acts, grads[step], base + spot, spot, size)
        ring, ring_at, swap, swap_at = returned[step]
        ref, at = (ring, ring_at + spot) if where == "ring" else (swap, swap_at + spot)
        return ref[at : at + size, :]

    def natural(offset, b, tile, there):
        live = (b * UNIT + line < here) & (columns < there)
        out[offset, b * UNIT : (b + 1) * UNIT, :] = jnp.where(live, tile.T, 0.0)

    def arrival(offset, c, tile, there):
        token_at = (line // SUB) * UNIT + c * SUB + line % SUB
        tile = jnp.where((token_at < here) & (columns < there), tile.T, 0.0)
        for q in range(WID):
            first = q * UNIT + c * SUB
            out[offset, first : first + SUB, :] = tile[q * SUB : (q + 1) * SUB]

    there = [lengths_ref[lax.rem(token + offset + total - 2, total)] for offset in range(5)]
    for c in range(units):
        arrival(0, c, block("ring", ("rt", c), c), there[0])
        tt = [jnp.concatenate([block(r, ("tt", a, c), max(a, c)) for a in range(units)], axis=0) for r in ("ring", "local")]
        arrival(1, c, jnp.where(even, tt[0], tt[1]), there[1])
        arrival(3, c, jnp.concatenate([block("swap", ("tj", a, c), max(a, c)) for a in range(units)], axis=0), there[3])
    for b in range(WID):
        natural(2, b, product(selves, selves, b * UNIT, (WID + b) * UNIT, UNIT), there[2])
        natural(4, b, jnp.concatenate([block("local", ("rj", c, b), c) for c in range(units)], axis=0), there[4])


def shards(acts, grads, lengths):
    rows = acts.shape[0]
    units = rows // UNIT
    length = lax.axis_size("tok")
    token = lax.axis_index("tok")
    width = lax.axis_index("wid")
    place = jnp.stack([token % 2, width % 2, width // 2, width, token]).astype(jnp.int32)
    swap = [(i, i ^ 1) for i in range(length)]
    down = [(i, (i - 2) % length) for i in range(length)]
    up = [(i, (i + 2) % length) for i in range(length)]
    layouts = [step_layout(c, units) for c in range(units)]

    def floats(n):
        return (jax.ShapeDtypeStruct((2, n, UNIT), jnp.float32),) * 2

    def over_core(send):
        return lax.ppermute(send, "wid", [(w, w ^ 1) for w in range(WID)])

    own_g = grads.T
    mine = list(call(reorder_kernel, (jax.ShapeDtypeStruct((grads.shape[1], UNIT), jnp.bfloat16),) * units, own_g))
    alive = jnp.max(lengths) > 0
    seen = {}

    def after(x, names):
        if not names:
            return x
        x, *held = lax.optimization_barrier((x, *[seen[name] for name in names]))
        seen.update(zip(names, held))
        return x

    def start(name, chunk):
        seen["R" + name] = lax.ppermute(after(chunk, GATES.get("R" + name)), "tok", down)
        seen["O" + name] = lax.ppermute(after(chunk, GATES.get("O" + name)), "tok", swap)

    def exchange(name, kernel, n, first, *rest):
        def summed(*args):
            keep, send = call(kernel, floats(n), place, *args, scalars=1)
            arrived = over_core(send)
            return keep[0] + arrived[0], keep[1] + arrived[1]

        def nothing(*args):
            return (jnp.zeros((n, UNIT), jnp.float32),) * 2

        first = after(first, GATES.get("K" + name))
        if name in PLAIN:
            near, far = summed(first, *rest)
        else:
            near, far = lax.cond(alive, summed, nothing, first, *rest)
        seen["S" + name] = lax.ppermute(after(far, GATES.get("S" + name)), "wid", [(w, w ^ 2) for w in range(WID)])
        return near

    def pair(c):
        if str(c) in PIECES:
            return seen["R%d" % c], seen["O%d" % c]
        return tuple(jnp.concatenate([seen["%s%d%s" % (side, c, half)] for half in "ab"], axis=0) for side in "RO")

    near = {}
    for piece in PIECES:
        if piece == "A":
            start(piece, acts)
        elif piece[0] in "0123":
            chunk = mine[int(piece[0])]
            cut = chunk.shape[0] // 2
            start(piece, {"": chunk, "a": chunk[:cut], "b": chunk[cut:]}[piece[1:]])
        elif piece == "kS":
            near["S"] = exchange("S", self_kernel, 2 * WID * UNIT, acts, own_g)
        elif piece == "kA":
            everything = sum(size for _, _, _, size in layouts)
            near["A"] = exchange("A", lambda *refs: acts_kernel(layouts, *refs), everything, acts, seen["RA"], seen["OA"])
        else:
            c = int(piece[1])
            spot, size = layouts[c][0], layouts[c][3]
            pairs = [pair(a) for a in range(c + 1)]
            near[c] = seen["N%d" % c] = exchange(
                piece[1], lambda *refs, c=c, spot=spot: grads_kernel(c, spot, *refs),
                size, own_g, *mine[: c + 1], *[p[0] for p in pairs], *[p[1] for p in pairs],
            )

    returned = []
    for i, steps in enumerate(GROUPS):
        sizes = [sum(layouts[c][1] for c in steps), sum(layouts[c][2] - layouts[c][1] for c in steps)]
        first = after(near[steps[0]], GATES.get("G%d" % i))
        grams = sum([[first if c == steps[0] else near[c], seen["S%d" % c]] for c in steps], [])
        ring, swapped = call(
            lambda *refs, steps=steps: return_kernel(layouts, steps, *refs),
            tuple(jax.ShapeDtypeStruct((n, UNIT), jnp.float32) for n in sizes),
            near["A"], seen["SA"], *grams,
        )
        returned += [lax.ppermute(ring, "tok", up), lax.ppermute(swapped, "tok", swap)]

    grams = sum([[near[c], seen["S%d" % c]] for c in range(units)], [])
    out = call(
        lambda *refs: final_kernel(layouts, GROUPS, *refs),
        jax.ShapeDtypeStruct((5, rows, UNIT), jnp.float32),
        place, lengths, near["S"], seen["SS"], near["A"], seen["SA"], *grams, *returned, scalars=2,
    )
    return out.transpose(1, 0, 2)


def solution(mesh):
    return jax.shard_map(
        shards,
        mesh=mesh,
        in_specs=(P("tok", "wid"), P("tok", "wid"), P()),
        out_specs=P("tok", None, "wid"),
        check_vma=False,
    )
```

```python
import math

import jax
import jax.numpy as jnp
from jax import lax
from jax.experimental import pallas as pl
from jax.experimental.pallas import tpu as pltpu
from jax.sharding import PartitionSpec as P

D = 4096
FF = 11008
WID = 4
UNIT = 128
SUB = UNIT // WID
VMEM_LIMIT = 24 << 20
PIECES = ['A', '0', 'kS', '1', 'kA', '2', '3', 'k0', 'k1', 'k2', 'k3']
GATES = {'R1': ['RA'], 'O1': ['OA'], 'R2': ['RA'], 'O2': ['OA'], 'R3': ['R1'], 'O3': ['O1'], 'KA': ['SS'], 'K0': ['SS'], 'K1': ['SA'], 'K2': ['S0'], 'K3': ['S0', 'S1'], 'SA': [], 'S0': ['SA'], 'S1': [], 'S2': [], 'S3': ['S0', 'S1'], 'G0': [], 'G1': []}
PLAIN = []
GROUPS = [[0, 1, 2], [3]]
SMEM = pl.BlockSpec(memory_space=pltpu.SMEM)
VMEM = pl.BlockSpec(memory_space=pltpu.VMEM)


def call(kernel, outs, *args, scalars=0, memory=VMEM, scratch=()):
    return pl.pallas_call(
        kernel,
        out_shape=outs,
        in_specs=[SMEM] * scalars + [memory] * (len(args) - scalars),
        out_specs=jax.tree.map(lambda _: VMEM, outs),
        scratch_shapes=scratch,
        cost_estimate=pl.CostEstimate(flops=2000000000, bytes_accessed=2000000, transcendentals=0),
        compiler_params=pltpu.CompilerParams(vmem_limit_bytes=VMEM_LIMIT),
    )(*args)


def dot(left, right, dims):
    return lax.dot_general(left, right, (dims, ((), ())), preferred_element_type=jnp.float32)


def row_dot(left, right):
    return dot(left, right, ((1,), (1,)))


def put(place_ref, keep, send, at, quarters):
    core = place_ref[1] == 0
    side = place_ref[2] == 0
    rows = pl.ds(at, quarters[0].shape[0])
    kept = [jnp.where(core, quarters[2 * s], quarters[2 * s + 1]) for s in range(2)]
    sent = [jnp.where(core, quarters[2 * s + 1], quarters[2 * s]) for s in range(2)]
    for ref, pair in ((keep, kept), (send, sent)):
        ref[0, rows, :] = jnp.where(side, pair[0], pair[1])
        ref[1, rows, :] = jnp.where(side, pair[1], pair[0])


def split_rows(block):
    n = block.shape[0] // WID
    return [block[q * n : (q + 1) * n] for q in range(WID)]


def lanes(block, b):
    return block[:, b * UNIT : (b + 1) * UNIT]


def step_layout(step, units):
    fresh = [(step, b) for b in range(step + 1)] + [(a, step) for a in range(step)]
    at, spot = UNIT, {("rt", step): 0}
    for a, b in fresh:
        spot[("tt", b, a)] = at
        at += SUB
    n_ring = at
    for a, b in fresh:
        spot[("tj", a, b)] = at
        at += SUB
    n_swap = at
    for b in range(WID):
        spot[("rj", step, b)] = at
        at += SUB
    return spot, n_ring, n_swap, at


def put_ring(place_ref, keep, send, spot, base, step, block):
    columns = [lanes(block, b) for b in range(WID)]
    put(place_ref, keep, send, base + spot[("rt", step)], [c.T for c in columns])
    for b in range(WID):
        put(place_ref, keep, send, base + spot[("rj", step, b)], split_rows(columns[b]))


def put_third(place_ref, keep, send, spot, base, a, b, block):
    put(place_ref, keep, send, base + spot[("tj", a, b)], split_rows(block))
    put(place_ref, keep, send, base + spot[("tt", b, a)], split_rows(block.T))


def reorder_kernel(g_ref, *outs):
    units = len(outs)
    tokens = g_ref.shape[1]
    source = lax.broadcasted_iota(jnp.int32, (tokens, UNIT), 0)
    lane = lax.broadcasted_iota(jnp.int32, (tokens, UNIT), 1)
    for c, out in enumerate(outs):
        wanted = (lane // SUB) * UNIT + c * SUB + lane % SUB
        pick = jnp.where(source == wanted, 1.0, 0.0).astype(jnp.bfloat16)
        out[...] = dot(g_ref[...], pick, ((1,), (0,))).astype(jnp.bfloat16)


def self_kernel(place_ref, a_ref, g_ref, keep, send):
    acts = a_ref[...]
    grads = g_ref[...]
    for i, block in enumerate((row_dot(acts, acts), dot(grads.T, grads, ((1,), (0,))))):
        for b in range(WID):
            put(place_ref, keep, send, (i * WID + b) * UNIT, split_rows(lanes(block, b)))


def acts_kernel(layouts, place_ref, own_ref, ring_ref, other_ref, keep, send):
    units = len(layouts)
    even = place_ref[0] == 0

    def arrival(x):
        return jnp.concatenate([x[q * UNIT + c * SUB : q * UNIT + (c + 1) * SUB] for c in range(units) for q in range(WID)], axis=0)

    own, ring, other = own_ref[...], ring_ref[...], other_ref[...]
    chosen = arrival(jnp.where(even, ring, own))
    ring = arrival(ring)
    other = arrival(other)
    base = 0
    for c, (spot, _, _, size) in enumerate(layouts):
        put_ring(place_ref, keep, send, spot, base, c, row_dot(ring[c * UNIT : (c + 1) * UNIT], own))
        base += size
    for a in range(units):
        block = row_dot(chosen[a * UNIT : (a + 1) * UNIT], other)
        for b in range(units):
            step = max(a, b)
            base = sum(layouts[s][3] for s in range(step))
            put_third(place_ref, keep, send, layouts[step][0], base, a, b, lanes(block, b))


def grads_kernel(step, spot, place_ref, own_hbm, *refs):
    n = step + 1
    mine, ring, other, (keep, send, own, fresh, chosen, others, sems) = refs[:n], refs[n : 2 * n], refs[2 * n : 3 * n], refs[3 * n :]
    even = place_ref[0] == 0
    half = own.shape[0] // 2

    def column(ref, a):
        return ref.at[:, a * UNIT : (a + 1) * UNIT]

    copies = [
        pltpu.make_async_copy(ring[step], fresh, sems.at[0]),
        pltpu.make_async_copy(own_hbm.at[:half], own.at[:half], sems.at[1]),
        pltpu.make_async_copy(own_hbm.at[half:], own.at[half:], sems.at[2]),
    ]
    third = [pltpu.make_async_copy(other[a], column(others, a), sems.at[3 + a]) for a in range(n)]
    from_ring = [pltpu.make_async_copy(ring[a], column(chosen, a), sems.at[3 + n + a]) for a in range(n)]
    from_mine = [pltpu.make_async_copy(mine[a], column(chosen, a), sems.at[3 + n + a]) for a in range(n)]
    for copy in copies:
        copy.start()

    @pl.when(even)
    def _():
        for copy in from_ring:
            copy.start()

    @pl.when(jnp.logical_not(even))
    def _():
        for copy in from_mine:
            copy.start()

    for copy in third:
        copy.start()
    for copy in copies:
        copy.wait()
    put_ring(place_ref, keep, send, spot, 0, step, dot(fresh[...].T, own[...], ((1,), (0,))))
    for copy in from_ring + third:
        copy.wait()
    block = dot(column(chosen, step)[...].T, others[...], ((1,), (0,)))
    for b in range(n):
        put_third(place_ref, keep, send, spot, 0, step, b, lanes(block, b))
    if step:
        block = dot(column(others, step)[...].T, chosen[:, : step * UNIT], ((1,), (0,))).T
        for a in range(step):
            put_third(place_ref, keep, send, spot, 0, a, step, block[a * UNIT : (a + 1) * UNIT])


def grads_scratch(own, n):
    deep = own.shape[0]
    arrays = [pltpu.VMEM((deep, width), jnp.bfloat16) for width in (own.shape[1], UNIT, n * UNIT, n * UNIT)]
    return (*arrays, pltpu.SemaphoreType.DMA((3 + 2 * n,)))


def product(acts, grads, act_at, grad_at, rows):
    act_sum = acts[0][act_at : act_at + rows, :] + acts[1][act_at : act_at + rows, :]
    grad_sum = grads[0][grad_at : grad_at + rows, :] + grads[1][grad_at : grad_at + rows, :]
    return (act_sum * (1.0 / math.sqrt(D))) * (grad_sum * (1.0 / math.sqrt(FF)))


def return_kernel(layouts, steps, *refs):
    acts, (ring, swap) = refs[:2], refs[-2:]
    ring_at = swap_at = 0
    for i, c in enumerate(steps):
        grads = refs[2 + 2 * i : 4 + 2 * i]
        _, n_ring, n_swap, _ = layouts[c]
        base = sum(layouts[s][3] for s in range(c))
        ring[ring_at : ring_at + n_ring, :] = product(acts, grads, base, 0, n_ring)
        swap[swap_at : swap_at + n_swap - n_ring, :] = product(acts, grads, base + n_ring, n_ring, n_swap - n_ring)
        ring_at += n_ring
        swap_at += n_swap - n_ring


def final_kernel(layouts, groups, place_ref, lengths_ref, *refs):
    units = len(layouts)
    selves, acts, out = refs[:2], refs[2:4], refs[-1]
    grads = [refs[4 + 2 * c : 6 + 2 * c] for c in range(units)]
    returned = {}
    for i, steps in enumerate(groups):
        ring, swap = refs[4 + 2 * units + 2 * i : 6 + 2 * units + 2 * i]
        ring_at = swap_at = 0
        for c in steps:
            _, n_ring, n_swap, _ = layouts[c]
            returned[c] = ring, ring_at, swap, swap_at - n_ring
            ring_at += n_ring
            swap_at += n_swap - n_ring
    even = place_ref[0] == 0
    width = place_ref[3]
    token = place_ref[4]
    total = lengths_ref.shape[0]
    here = lengths_ref[token]
    columns = width * UNIT + lax.broadcasted_iota(jnp.int32, (UNIT, UNIT), 1)
    line = lax.broadcasted_iota(jnp.int32, (UNIT, UNIT), 0)

    def block(where, name, step):
        spot = layouts[step][0][name]
        size = UNIT if name[0] == "rt" else SUB
        if where == "local":
            base = sum(layouts[s][3] for s in range(step))
            return product(acts, grads[step], base + spot, spot, size)
        ring, ring_at, swap, swap_at = returned[step]
        ref, at = (ring, ring_at + spot) if where == "ring" else (swap, swap_at + spot)
        return ref[at : at + size, :]

    def natural(offset, b, tile, there):
        live = (b * UNIT + line < here) & (columns < there)
        out[offset, b * UNIT : (b + 1) * UNIT, :] = jnp.where(live, tile.T, 0.0)

    def arrival(offset, c, tile, there):
        token_at = (line // SUB) * UNIT + c * SUB + line % SUB
        tile = jnp.where((token_at < here) & (columns < there), tile.T, 0.0)
        for q in range(WID):
            first = q * UNIT + c * SUB
            out[offset, first : first + SUB, :] = tile[q * SUB : (q + 1) * SUB]

    there = [lengths_ref[lax.rem(token + offset + total - 2, total)] for offset in range(5)]
    for c in range(units):
        arrival(0, c, block("ring", ("rt", c), c), there[0])
        tt = [jnp.concatenate([block(r, ("tt", a, c), max(a, c)) for a in range(units)], axis=0) for r in ("ring", "local")]
        arrival(1, c, jnp.where(even, tt[0], tt[1]), there[1])
        arrival(3, c, jnp.concatenate([block("swap", ("tj", a, c), max(a, c)) for a in range(units)], axis=0), there[3])
    for b in range(WID):
        natural(2, b, product(selves, selves, b * UNIT, (WID + b) * UNIT, UNIT), there[2])
        natural(4, b, jnp.concatenate([block("local", ("rj", c, b), c) for c in range(units)], axis=0), there[4])


def shards(acts, grads, lengths):
    rows = acts.shape[0]
    units = rows // UNIT
    length = lax.axis_size("tok")
    token = lax.axis_index("tok")
    width = lax.axis_index("wid")
    place = jnp.stack([token % 2, width % 2, width // 2, width, token]).astype(jnp.int32)
    swap = [(i, i ^ 1) for i in range(length)]
    down = [(i, (i - 2) % length) for i in range(length)]
    up = [(i, (i + 2) % length) for i in range(length)]
    layouts = [step_layout(c, units) for c in range(units)]

    def floats(n):
        return (jax.ShapeDtypeStruct((2, n, UNIT), jnp.float32),) * 2

    def over_core(send):
        return lax.ppermute(send, "wid", [(w, w ^ 1) for w in range(WID)])

    own_g = grads.T
    mine = list(call(reorder_kernel, (jax.ShapeDtypeStruct((grads.shape[1], UNIT), jnp.bfloat16),) * units, own_g))
    alive = jnp.max(lengths) > 0
    seen = {}

    def after(x, names):
        if not names:
            return x
        x, *held = lax.optimization_barrier((x, *[seen[name] for name in names]))
        seen.update(zip(names, held))
        return x

    def start(name, chunk):
        seen["R" + name] = lax.ppermute(after(chunk, GATES.get("R" + name)), "tok", down)
        seen["O" + name] = lax.ppermute(after(chunk, GATES.get("O" + name)), "tok", swap)

    def exchange(name, kernel, n, first, *rest, **options):
        def summed(*args):
            keep, send = call(kernel, floats(n), place, *args, scalars=1, **options)
            arrived = over_core(send)
            return keep[0] + arrived[0], keep[1] + arrived[1]

        def nothing(*args):
            return (jnp.zeros((n, UNIT), jnp.float32),) * 2

        first = after(first, GATES.get("K" + name))
        if name in PLAIN:
            near, far = summed(first, *rest)
        else:
            near, far = lax.cond(alive, summed, nothing, first, *rest)
        seen["S" + name] = lax.ppermute(after(far, GATES.get("S" + name)), "wid", [(w, w ^ 2) for w in range(WID)])
        return near

    def pair(c):
        if str(c) in PIECES:
            return seen["R%d" % c], seen["O%d" % c]
        return tuple(jnp.concatenate([seen["%s%d%s" % (side, c, half)] for half in "ab"], axis=0) for side in "RO")

    near = {}
    for piece in PIECES:
        if piece == "A":
            start(piece, acts)
        elif piece[0] in "0123":
            chunk = mine[int(piece[0])]
            cut = chunk.shape[0] // 2
            start(piece, {"": chunk, "a": chunk[:cut], "b": chunk[cut:]}[piece[1:]])
        elif piece == "kS":
            near["S"] = exchange("S", self_kernel, 2 * WID * UNIT, acts, own_g)
        elif piece == "kA":
            everything = sum(size for _, _, _, size in layouts)
            near["A"] = exchange("A", lambda *refs: acts_kernel(layouts, *refs), everything, acts, seen["RA"], seen["OA"])
        else:
            c = int(piece[1])
            spot, size = layouts[c][0], layouts[c][3]
            pairs = [pair(a) for a in range(c + 1)]
            near[c] = seen["N%d" % c] = exchange(
                piece[1], lambda *refs, c=c, spot=spot: grads_kernel(c, spot, *refs),
                size, own_g, *mine[: c + 1], *[p[0] for p in pairs], *[p[1] for p in pairs],
                memory=pl.BlockSpec(memory_space=pl.ANY), scratch=grads_scratch(own_g, c + 1),
            )

    returned = []
    for i, steps in enumerate(GROUPS):
        sizes = [sum(layouts[c][1] for c in steps), sum(layouts[c][2] - layouts[c][1] for c in steps)]
        first = after(near[steps[0]], GATES.get("G%d" % i))
        grams = sum([[first if c == steps[0] else near[c], seen["S%d" % c]] for c in steps], [])
        ring, swapped = call(
            lambda *refs, steps=steps: return_kernel(layouts, steps, *refs),
            tuple(jax.ShapeDtypeStruct((n, UNIT), jnp.float32) for n in sizes),
            near["A"], seen["SA"], *grams,
        )
        returned += [lax.ppermute(ring, "tok", up), lax.ppermute(swapped, "tok", swap)]

    grams = sum([[near[c], seen["S%d" % c]] for c in range(units)], [])
    out = call(
        lambda *refs: final_kernel(layouts, GROUPS, *refs),
        jax.ShapeDtypeStruct((5, rows, UNIT), jnp.float32),
        place, lengths, near["S"], seen["SS"], near["A"], seen["SA"], *grams, *returned, scalars=2,
    )
    return out.transpose(1, 0, 2)


def solution(mesh):
    return jax.shard_map(
        shards,
        mesh=mesh,
        in_specs=(P("tok", "wid"), P("tok", "wid"), P()),
        out_specs=P("tok", None, "wid"),
        check_vma=False,
    )
```

```python
import math

import jax
import jax.numpy as jnp
from jax import lax
from jax.experimental import pallas as pl
from jax.experimental.pallas import tpu as pltpu
from jax.sharding import PartitionSpec as P

D = 4096
FF = 11008
WID = 4
UNIT = 128
SUB = UNIT // WID
WHOLE = 3
VMEM_LIMIT = 24 << 20
PIECES = ["A", "0", "kS", "1", "kA", "2", "3", "k0", "4", "k1", "k2", "k3", "k4"]
GATES = {"R1": ["RA"], "O1": ["OA"], "R2": ["RA"], "O2": ["OA"], "R3": ["R1"], "O3": ["O1"], "R4": ["R2"], "O4": ["O2"], "KA": ["SS"], "K0": ["SS"], "K1": ["SA"], "K2": ["S0"], "K3": ["S0", "S1"], "K4": ["S1"], "S0": ["SA"]}
PLAIN = []
GROUPS = [[0, 1, 2, 3], [4]]
SMEM = pl.BlockSpec(memory_space=pltpu.SMEM)
VMEM = pl.BlockSpec(memory_space=pltpu.VMEM)


def call(kernel, outs, *args, scalars=0, memory=VMEM, scratch=()):
    return pl.pallas_call(
        kernel,
        out_shape=outs,
        in_specs=[SMEM] * scalars + [memory] * (len(args) - scalars),
        out_specs=jax.tree.map(lambda _: VMEM, outs),
        scratch_shapes=scratch,
        cost_estimate=pl.CostEstimate(flops=0, bytes_accessed=0, transcendentals=0),
        compiler_params=pltpu.CompilerParams(vmem_limit_bytes=VMEM_LIMIT),
    )(*args)


def dot(left, right, dims):
    return lax.dot_general(left, right, (dims, ((), ())), preferred_element_type=jnp.float32)


def row_dot(left, right):
    return dot(left, right, ((1,), (1,)))


def put(place_ref, keep, send, at, quarters):
    core = place_ref[1] == 0
    side = place_ref[2] == 0
    rows = pl.ds(at, quarters[0].shape[0])
    kept = [jnp.where(core, quarters[2 * s], quarters[2 * s + 1]) for s in range(2)]
    sent = [jnp.where(core, quarters[2 * s + 1], quarters[2 * s]) for s in range(2)]
    for ref, pair in ((keep, kept), (send, sent)):
        ref[0, rows, :] = jnp.where(side, pair[0], pair[1])
        ref[1, rows, :] = jnp.where(side, pair[1], pair[0])


def split_rows(block):
    n = block.shape[0] // WID
    return [block[q * n : (q + 1) * n] for q in range(WID)]


def lanes(block, b):
    return block[:, b * UNIT : (b + 1) * UNIT]


def step_layouts():
    layouts = []
    for step in range(WHOLE + 2):
        half = step - WHOLE
        if half < 0:
            names = [(step, b) for b in range(step + 1)] + [(a, step) for a in range(step)]
            rt, size = UNIT, SUB
        else:
            names = [(step, b) for b in range(WHOLE)] + [(step, "p")] + [(a, step) for a in range(WHOLE)] + [("p", step)] * half
            rt, size = UNIT // 2, SUB // 2
        tt = [(("tt", b, a), size) for a, b in names]
        tj = [(("tj", a, b), size) for a, b in names]
        rj = [(("rj", step, b), size) for b in range(WID)]
        spot, at, ends = {}, 0, []
        for part in ([(("rt", step), rt)] + tt, tj, rj):
            for name, rows in part:
                spot[name] = (at, rows)
                at += rows
            ends.append(at)
        layouts.append((spot, *ends))
    return layouts


def pack(block):
    n = block.shape[0] // 2
    return jnp.concatenate([block[:n], block[n:]], axis=1)


def unpack(block):
    return jnp.concatenate([block[:, : UNIT // 2], block[:, UNIT // 2 :]], axis=0)


def put_ring(place_ref, keep, send, spot, base, step, block):
    columns = [lanes(block, b) for b in range(WID)]
    quarters = [pack(c.T) if step >= WHOLE else c.T for c in columns]
    put(place_ref, keep, send, base + spot[("rt", step)][0], quarters)
    for b in range(WID):
        put(place_ref, keep, send, base + spot[("rj", step, b)][0], split_rows(columns[b]))


def put_third(place_ref, keep, send, spot, base, a, b, block):
    put(place_ref, keep, send, base + spot[("tj", a, b)][0], split_rows(block))
    put(place_ref, keep, send, base + spot[("tt", b, a)][0], split_rows(block.T))


def put_half(place_ref, keep, send, spot, base, first, second, tall, wide, block):
    put(place_ref, keep, send, base + spot[(tall, first, second)][0], split_rows(block))
    turned = block.T
    if second == "p":
        parts = [split_rows(x) for x in (turned[: UNIT // 2], turned[UNIT // 2 :])]
        quarters = [jnp.concatenate([parts[0][q], parts[1][q]], axis=0) for q in range(WID)]
    else:
        quarters = split_rows(turned)
    put(place_ref, keep, send, base + spot[(wide, second, first)][0], [pack(q) for q in quarters])


def put_halves(place_ref, keep, send, spot, base, step, by_chosen, by_other):
    for b in range(WHOLE):
        put_half(place_ref, keep, send, spot, base, step, b, "tj", "tt", lanes(by_chosen, b))
        put_half(place_ref, keep, send, spot, base, step, b, "tt", "tj", lanes(by_other, b))
    put_half(place_ref, keep, send, spot, base, step, "p", "tj", "tt", lanes(by_chosen, WHOLE))
    if step > WHOLE:
        put_half(place_ref, keep, send, spot, base, step, "p", "tt", "tj", lanes(by_other, WHOLE))


def reorder_kernel(g_ref, *outs):
    tokens = g_ref.shape[1]
    half = g_ref.shape[0] // 2
    source = lax.broadcasted_iota(jnp.int32, (tokens, UNIT), 0)
    lane = lax.broadcasted_iota(jnp.int32, (tokens, UNIT), 1)

    def pick(wanted):
        return jnp.where(source == wanted, 1.0, 0.0).astype(jnp.bfloat16)

    for c in range(WHOLE):
        wanted = (lane // SUB) * UNIT + c * SUB + lane % SUB
        outs[c][...] = dot(g_ref[...], pick(wanted), ((1,), (0,))).astype(jnp.bfloat16)
    size = SUB // 2
    for h in range(2):
        inner = lane % (UNIT // 2)
        wanted = (inner // size) * UNIT + WHOLE * SUB + h * size + inner % size
        upper = dot(g_ref[:half, :], pick(jnp.where(lane < UNIT // 2, wanted, -1)), ((1,), (0,)))
        lower = dot(g_ref[half:, :], pick(jnp.where(lane < UNIT // 2, -1, wanted)), ((1,), (0,)))
        outs[WHOLE + h][...] = (upper + lower).astype(jnp.bfloat16)


def self_kernel(place_ref, a_ref, g_ref, keep, send):
    acts = a_ref[...]
    grads = g_ref[...]
    for i, block in enumerate((row_dot(acts, acts), dot(grads.T, grads, ((1,), (0,))))):
        for b in range(WID):
            put(place_ref, keep, send, (i * WID + b) * UNIT, split_rows(lanes(block, b)))


def acts_kernel(layouts, place_ref, own_ref, ring_ref, other_ref, keep, send):
    even = place_ref[0] == 0

    def arrival(x):
        spans = [(q * UNIT + c * SUB, SUB) for c in range(WHOLE) for q in range(WID)]
        spans += [(q * UNIT + WHOLE * SUB + h * (SUB // 2), SUB // 2) for h in range(2) for q in range(WID)]
        return jnp.concatenate([x[at : at + size] for at, size in spans], axis=0)

    own, ring, other = own_ref[...], ring_ref[...], other_ref[...]
    chosen = arrival(jnp.where(even, ring, own))
    ring = row_dot(arrival(ring), own)
    third = row_dot(chosen, arrival(other))
    base = 0
    for c, layout in enumerate(layouts):
        spot = layout[0]
        if c < WHOLE:
            rows = slice(c * UNIT, (c + 1) * UNIT)
            put_ring(place_ref, keep, send, spot, base, c, ring[rows])
            for b in range(c + 1):
                put_third(place_ref, keep, send, spot, base, c, b, lanes(third[rows], b))
            for a in range(c):
                put_third(place_ref, keep, send, spot, base, a, c, lanes(third[a * UNIT : (a + 1) * UNIT], c))
        else:
            first = (c - WHOLE) * (UNIT // 2)
            rows = slice(WHOLE * UNIT + first, WHOLE * UNIT + first + UNIT // 2)
            put_ring(place_ref, keep, send, spot, base, c, ring[rows])
            by_other = lanes(third, WHOLE).T[first : first + UNIT // 2]
            put_halves(place_ref, keep, send, spot, base, c, third[rows], by_other)
        base += layout[3]


def grads_kernel(step, spot, place_ref, own_hbm, *refs):
    n = step + 1
    mine, ring, other, (keep, send, own, fresh, chosen, others, sems) = refs[:n], refs[n : 2 * n], refs[2 * n : 3 * n], refs[3 * n :]
    even = place_ref[0] == 0
    half = own.shape[0] // 2

    def column(ref, a):
        return ref.at[:, a * UNIT : (a + 1) * UNIT]

    copies = [
        pltpu.make_async_copy(ring[step], fresh, sems.at[0]),
        pltpu.make_async_copy(own_hbm.at[:half], own.at[:half], sems.at[1]),
        pltpu.make_async_copy(own_hbm.at[half:], own.at[half:], sems.at[2]),
    ]
    third = [pltpu.make_async_copy(other[a], column(others, a), sems.at[3 + a]) for a in range(n)]
    from_ring = [pltpu.make_async_copy(ring[a], column(chosen, a), sems.at[3 + n + a]) for a in range(n)]
    from_mine = [pltpu.make_async_copy(mine[a], column(chosen, a), sems.at[3 + n + a]) for a in range(n)]
    for copy in copies:
        copy.start()

    @pl.when(even)
    def _():
        for copy in from_ring:
            copy.start()

    @pl.when(jnp.logical_not(even))
    def _():
        for copy in from_mine:
            copy.start()

    for copy in third:
        copy.start()
    for copy in copies:
        copy.wait()
    put_ring(place_ref, keep, send, spot, 0, step, dot(fresh[...].T, own[...], ((1,), (0,))))
    for copy in from_ring + third:
        copy.wait()
    block = dot(column(chosen, step)[...].T, others[...], ((1,), (0,)))
    for b in range(n):
        put_third(place_ref, keep, send, spot, 0, step, b, lanes(block, b))
    if step:
        block = dot(column(others, step)[...].T, chosen[:, : step * UNIT], ((1,), (0,))).T
        for a in range(step):
            put_third(place_ref, keep, send, spot, 0, a, step, block[a * UNIT : (a + 1) * UNIT])


def halves_kernel(step, spot, place_ref, own_hbm, *refs):
    n = step - WHOLE + 1
    count = WHOLE + n
    mine, ring, other, scratch = refs[:count], refs[count : 2 * count], refs[2 * count : 3 * count], refs[3 * count :]
    keep, send, own, fresh, chosen, others, chosen_part, other_part, sems = scratch
    even = place_ref[0] == 0
    deep = own.shape[0] // 2
    size = UNIT // 2

    def home(whole, part, a):
        return whole.at[:, a * UNIT : (a + 1) * UNIT] if a < WHOLE else part.at[a - WHOLE]

    copies = [
        pltpu.make_async_copy(ring[step], fresh, sems.at[0]),
        pltpu.make_async_copy(own_hbm.at[:deep], own.at[:deep], sems.at[1]),
        pltpu.make_async_copy(own_hbm.at[deep:], own.at[deep:], sems.at[2]),
    ]
    third = [pltpu.make_async_copy(other[a], home(others, other_part, a), sems.at[3 + a]) for a in range(count)]
    from_ring = [pltpu.make_async_copy(ring[a], home(chosen, chosen_part, a), sems.at[3 + count + a]) for a in range(count)]
    from_mine = [pltpu.make_async_copy(mine[a], home(chosen, chosen_part, a), sems.at[3 + count + a]) for a in range(count)]
    for copy in copies:
        copy.start()

    @pl.when(even)
    def _():
        for copy in from_ring:
            copy.start()

    @pl.when(jnp.logical_not(even))
    def _():
        for copy in from_mine:
            copy.start()

    for copy in third:
        copy.start()

    def against(turned, right):
        return dot(turned[:size], right[:deep, :], ((1,), (0,))) + dot(turned[size:], right[deep:, :], ((1,), (0,)))

    def against_half(turned, right):
        return dot(turned[:size], right, ((1,), (0,)))[:, :size] + dot(turned[size:], right, ((1,), (0,)))[:, size:]

    def product_of(turned, whole, part):
        halves = [against_half(turned, part[h]) for h in range(n)]
        return jnp.concatenate([against(turned, whole), halves[0], halves[-1]], axis=1)

    for copy in copies:
        copy.wait()
    put_ring(place_ref, keep, send, spot, 0, step, against(fresh[...].T, own))
    for copy in from_ring + third:
        copy.wait()
    by_chosen = product_of(chosen_part[n - 1].T, others, other_part)
    by_other = product_of(other_part[n - 1].T, chosen, chosen_part)
    put_halves(place_ref, keep, send, spot, 0, step, by_chosen, by_other)


def halves_scratch(own, n):
    deep = own.shape[0]
    arrays = [pltpu.VMEM((deep, own.shape[1]), jnp.bfloat16), pltpu.VMEM((deep // 2, UNIT), jnp.bfloat16)]
    arrays += [pltpu.VMEM((deep, WHOLE * UNIT), jnp.bfloat16)] * 2 + [pltpu.VMEM((n, deep // 2, UNIT), jnp.bfloat16)] * 2
    return (*arrays, pltpu.SemaphoreType.DMA((3 + 2 * (WHOLE + n),)))


def grads_scratch(own, n):
    deep = own.shape[0]
    arrays = [pltpu.VMEM((deep, width), jnp.bfloat16) for width in (own.shape[1], UNIT, n * UNIT, n * UNIT)]
    return (*arrays, pltpu.SemaphoreType.DMA((3 + 2 * n,)))


def product(acts, grads, act_at, grad_at, rows):
    act_sum = acts[0][act_at : act_at + rows, :] + acts[1][act_at : act_at + rows, :]
    grad_sum = grads[0][grad_at : grad_at + rows, :] + grads[1][grad_at : grad_at + rows, :]
    return (act_sum * (1.0 / math.sqrt(D))) * (grad_sum * (1.0 / math.sqrt(FF)))


def return_kernel(layouts, steps, *refs):
    acts, (ring, swap) = refs[:2], refs[-2:]
    ring_at = swap_at = 0
    for i, c in enumerate(steps):
        grads = refs[2 + 2 * i : 4 + 2 * i]
        _, n_ring, n_swap, _ = layouts[c]
        base = sum(layouts[s][3] for s in range(c))
        ring[ring_at : ring_at + n_ring, :] = product(acts, grads, base, 0, n_ring)
        swap[swap_at : swap_at + n_swap - n_ring, :] = product(acts, grads, base + n_ring, n_ring, n_swap - n_ring)
        ring_at += n_ring
        swap_at += n_swap - n_ring


def final_kernel(layouts, groups, place_ref, lengths_ref, *refs):
    count = len(layouts)
    selves, acts, out = refs[:2], refs[2:4], refs[-1]
    grads = [refs[4 + 2 * c : 6 + 2 * c] for c in range(count)]
    returned = {}
    for i, steps in enumerate(groups):
        ring, swap = refs[4 + 2 * count + 2 * i : 6 + 2 * count + 2 * i]
        ring_at = swap_at = 0
        for c in steps:
            _, n_ring, n_swap, _ = layouts[c]
            returned[c] = ring, ring_at, swap, swap_at - n_ring
            ring_at += n_ring
            swap_at += n_swap - n_ring
    even = place_ref[0] == 0
    width = place_ref[3]
    token = place_ref[4]
    total = lengths_ref.shape[0]
    here = lengths_ref[token]
    columns = width * UNIT + lax.broadcasted_iota(jnp.int32, (UNIT, UNIT), 1)
    line = lax.broadcasted_iota(jnp.int32, (UNIT, UNIT), 0)

    def block(where, *name):
        step = max(x for x in name[1 : 2 if name[0] == "rj" else 3] if x != "p")
        at, size = layouts[step][0][name]
        if where == "local":
            base = sum(layout[3] for layout in layouts[:step])
            return product(acts, grads[step], base + at, at, size)
        ring, ring_at, swap, swap_at = returned[step]
        ref, at = (ring, ring_at + at) if where == "ring" else (swap, swap_at + at)
        return ref[at : at + size, :]

    def beside(left, right):
        return jnp.concatenate([unpack(left), unpack(right)], axis=1)

    def third(where, kind, c):
        one, two = WHOLE, WHOLE + 1
        if c < WHOLE:
            rows = [block(where, kind, a, c) for a in (*range(WHOLE), one, two)]
        else:
            rows = [beside(block(where, kind, a, one), block(where, kind, a, two)) for a in range(WHOLE)]
            if kind == "tt":
                rows.append(beside(block(where, kind, "p", one), block(where, kind, "p", two))[: SUB // 2])
            else:
                crossed = unpack(block(where, kind, "p", two))[: SUB // 2]
                rows.append(jnp.concatenate([block(where, kind, one, "p")[:, : UNIT // 2], crossed], axis=1))
            rows.append(block(where, kind, two, "p"))
        return jnp.concatenate(rows, axis=0)

    def natural(offset, b, tile, there):
        live = (b * UNIT + line < here) & (columns < there)
        out[offset, b * UNIT : (b + 1) * UNIT, :] = jnp.where(live, tile.T, 0.0)

    def arrival(offset, c, tile, there):
        if c < WHOLE:
            token_at = (line // SUB) * UNIT + c * SUB + line % SUB
            spans = [(q * SUB, q * UNIT + c * SUB, SUB) for q in range(WID)]
        else:
            size = SUB // 2
            inner = line % (UNIT // 2)
            token_at = (inner // size) * UNIT + c * SUB + (line // (UNIT // 2)) * size + inner % size
            spans = [(h * (UNIT // 2) + q * size, q * UNIT + c * SUB + h * size, size) for h in range(2) for q in range(WID)]
        tile = jnp.where((token_at < here) & (columns < there), tile.T, 0.0)
        for at, first, size in spans:
            out[offset, first : first + size, :] = tile[at : at + size]

    there = [lengths_ref[lax.rem(token + offset + total - 2, total)] for offset in range(5)]
    for c in range(WHOLE + 1):
        rt = block("ring", "rt", c) if c < WHOLE else beside(block("ring", "rt", WHOLE), block("ring", "rt", WHOLE + 1))
        arrival(0, c, rt, there[0])
        arrival(1, c, jnp.where(even, third("ring", "tt", c), third("local", "tt", c)), there[1])
        arrival(3, c, third("swap", "tj", c), there[3])
    for b in range(WID):
        natural(2, b, product(selves, selves, b * UNIT, (WID + b) * UNIT, UNIT), there[2])
        natural(4, b, jnp.concatenate([block("local", "rj", c, b) for c in range(WHOLE + 2)], axis=0), there[4])


def shards(acts, grads, lengths):
    rows = acts.shape[0]
    length = lax.axis_size("tok")
    token = lax.axis_index("tok")
    width = lax.axis_index("wid")
    place = jnp.stack([token % 2, width % 2, width // 2, width, token]).astype(jnp.int32)
    swap = [(i, i ^ 1) for i in range(length)]
    down = [(i, (i - 2) % length) for i in range(length)]
    up = [(i, (i + 2) % length) for i in range(length)]
    layouts = step_layouts()

    def floats(n):
        return (jax.ShapeDtypeStruct((2, n, UNIT), jnp.float32),) * 2

    def over_core(send):
        return lax.ppermute(send, "wid", [(w, w ^ 1) for w in range(WID)])

    own_g = grads.T
    deep = grads.shape[1]
    shapes = [jax.ShapeDtypeStruct((deep if c < WHOLE else deep // 2, UNIT), jnp.bfloat16) for c in range(WHOLE + 2)]
    mine = call(reorder_kernel, tuple(shapes), own_g)
    alive = jnp.max(lengths) > 0
    seen = {}

    def after(x, names):
        if not names:
            return x
        x, *held = lax.optimization_barrier((x, *[seen[name] for name in names]))
        seen.update(zip(names, held))
        return x

    def start(name, chunk):
        seen["R" + name] = lax.ppermute(after(chunk, GATES.get("R" + name)), "tok", down)
        seen["O" + name] = lax.ppermute(after(chunk, GATES.get("O" + name)), "tok", swap)

    def exchange(name, kernel, n, first, *rest, **options):
        def summed(*args):
            keep, send = call(kernel, floats(n), place, *args, scalars=1, **options)
            arrived = over_core(send)
            return keep[0] + arrived[0], keep[1] + arrived[1]

        def nothing(*args):
            return (jnp.zeros((n, UNIT), jnp.float32),) * 2

        first = after(first, GATES.get("K" + name))
        if name in PLAIN:
            near, far = summed(first, *rest)
        else:
            near, far = lax.cond(alive, summed, nothing, first, *rest)
        seen["S" + name] = lax.ppermute(after(far, GATES.get("S" + name)), "wid", [(w, w ^ 2) for w in range(WID)])
        return near

    near = {}
    for piece in PIECES:
        if piece == "A":
            start(piece, acts)
        elif piece.isdigit():
            start(piece, mine[int(piece)])
        elif piece == "kS":
            near["S"] = exchange("S", self_kernel, 2 * WID * UNIT, acts, own_g)
        elif piece == "kA":
            everything = sum(size for _, _, _, size in layouts)
            near["A"] = exchange("A", lambda *refs: acts_kernel(layouts, *refs), everything, acts, seen["RA"], seen["OA"])
        else:
            c = int(piece[1])
            spot, size = layouts[c][0], layouts[c][3]
            kernel, scratch = grads_kernel, grads_scratch(own_g, c + 1)
            if c >= WHOLE:
                kernel, scratch = halves_kernel, halves_scratch(own_g, c - WHOLE + 1)
            arrived = [seen["%s%d" % (side, a)] for side in "RO" for a in range(c + 1)]
            near[c] = seen["N%d" % c] = exchange(
                piece[1], lambda *refs, c=c, spot=spot, kernel=kernel: kernel(c, spot, *refs),
                size, own_g, *mine[: c + 1], *arrived, memory=pl.BlockSpec(memory_space=pl.ANY), scratch=scratch,
            )

    returned = []
    for i, steps in enumerate(GROUPS):
        sizes = [sum(layouts[c][1] for c in steps), sum(layouts[c][2] - layouts[c][1] for c in steps)]
        first = after(near[steps[0]], GATES.get("G%d" % i))
        grams = sum([[first if c == steps[0] else near[c], seen["S%d" % c]] for c in steps], [])
        ring, swapped = call(
            lambda *refs, steps=steps: return_kernel(layouts, steps, *refs),
            tuple(jax.ShapeDtypeStruct((n, UNIT), jnp.float32) for n in sizes),
            near["A"], seen["SA"], *grams,
        )
        returned += [lax.ppermute(ring, "tok", up), lax.ppermute(swapped, "tok", swap)]

    grams = sum([[near[c], seen["S%d" % c]] for c in range(WHOLE + 2)], [])
    out = call(
        lambda *refs: final_kernel(layouts, GROUPS, *refs),
        jax.ShapeDtypeStruct((5, rows, UNIT), jnp.float32),
        place, lengths, near["S"], seen["SS"], near["A"], seen["SA"], *grams, *returned, scalars=2,
    )
    return out.transpose(1, 0, 2)


def solution(mesh):
    return jax.shard_map(
        shards,
        mesh=mesh,
        in_specs=(P("tok", "wid"), P("tok", "wid"), P()),
        out_specs=P("tok", None, "wid"),
        check_vma=False,
    )
```

```python
import math

import jax
import jax.numpy as jnp
from jax import lax
from jax.experimental import pallas as pl
from jax.experimental.pallas import tpu as pltpu
from jax.sharding import PartitionSpec as P

D = 4096
FF = 11008
WID = 4
UNIT = 128
SUB = UNIT // WID
WHOLE = 3
STEPS = ((0, 1), (2,), (3,), (4,))
HALVES = 2
VMEM_LIMIT = 24 << 20
PIECES = ["A", "0", "kS", "1", "kA", "2", "k0", "3", "k1", "k2", "k3"]
GATES = {"R1": ["RA"], "O1": ["OA"], "R2": ["RA"], "O2": ["OA"], "R3": ["R1"], "O3": ["O1"], "KA": ["SS"], "K0": ["SA"], "K1": ["S0"], "K2": ["S0"], "K3": ["S0"]}
PLAIN = []
GROUPS = [[0, 1, 2]]
SMEM = pl.BlockSpec(memory_space=pltpu.SMEM)
VMEM = pl.BlockSpec(memory_space=pltpu.VMEM)


def call(kernel, outs, *args, scalars=0, memory=VMEM, scratch=()):
    return pl.pallas_call(
        kernel,
        out_shape=outs,
        in_specs=[SMEM] * scalars + [memory] * (len(args) - scalars),
        out_specs=jax.tree.map(lambda _: VMEM, outs),
        scratch_shapes=scratch,
        cost_estimate=pl.CostEstimate(flops=0, bytes_accessed=0, transcendentals=0),
        compiler_params=pltpu.CompilerParams(vmem_limit_bytes=VMEM_LIMIT),
    )(*args)


def dot(left, right, dims):
    return lax.dot_general(left, right, (dims, ((), ())), preferred_element_type=jnp.float32)


def row_dot(left, right):
    return dot(left, right, ((1,), (1,)))


def put(place_ref, keep, send, at, quarters):
    core = place_ref[1] == 0
    side = place_ref[2] == 0
    rows = pl.ds(at, quarters[0].shape[0])
    kept = [jnp.where(core, quarters[2 * s], quarters[2 * s + 1]) for s in range(2)]
    sent = [jnp.where(core, quarters[2 * s + 1], quarters[2 * s]) for s in range(2)]
    for ref, pair in ((keep, kept), (send, sent)):
        ref[0, rows, :] = jnp.where(side, pair[0], pair[1])
        ref[1, rows, :] = jnp.where(side, pair[1], pair[0])


def split_rows(block):
    n = block.shape[0] // WID
    return [block[q * n : (q + 1) * n] for q in range(WID)]


def lanes(block, b):
    return block[:, b * UNIT : (b + 1) * UNIT]


def step_layouts():
    layouts = []
    for step, ids in enumerate(STEPS):
        if step < HALVES:
            names = [(c, b) for c in ids for b in range(ids[-1] + 1)] + [(a, c) for a in range(ids[0]) for c in ids]
            rt, size = UNIT, SUB
        else:
            c = ids[0]
            names = [(c, b) for b in range(WHOLE)] + [(c, "p")] + [(a, c) for a in range(WHOLE)] + [("p", c)] * (c - WHOLE)
            rt, size = UNIT // 2, SUB // 2
        parts = [(("rt", c), rt) for c in ids] + [(("tt", b, a), size) for a, b in names]
        parts = parts, [(("tj", a, b), size) for a, b in names], [(("rj", c, b), size) for c in ids for b in range(WID)]
        spot, at, ends = {}, 0, []
        for part in parts:
            for name, rows in part:
                spot[name] = (at, rows)
                at += rows
            ends.append(at)
        layouts.append((spot, *ends))
    return layouts


def pack(block):
    n = block.shape[0] // 2
    return jnp.concatenate([block[:n], block[n:]], axis=1)


def unpack(block):
    return jnp.concatenate([block[:, : UNIT // 2], block[:, UNIT // 2 :]], axis=0)


def put_ring(place_ref, keep, send, spot, base, c, block):
    columns = [lanes(block, b) for b in range(WID)]
    quarters = [pack(column.T) if c >= WHOLE else column.T for column in columns]
    put(place_ref, keep, send, base + spot[("rt", c)][0], quarters)
    for b in range(WID):
        put(place_ref, keep, send, base + spot[("rj", c, b)][0], split_rows(columns[b]))


def put_third(place_ref, keep, send, spot, base, a, b, block):
    put(place_ref, keep, send, base + spot[("tj", a, b)][0], split_rows(block))
    put(place_ref, keep, send, base + spot[("tt", b, a)][0], split_rows(block.T))


def put_half(place_ref, keep, send, spot, base, first, second, tall, wide, block):
    put(place_ref, keep, send, base + spot[(tall, first, second)][0], split_rows(block))
    turned = block.T
    if second == "p":
        parts = [split_rows(x) for x in (turned[: UNIT // 2], turned[UNIT // 2 :])]
        quarters = [jnp.concatenate([parts[0][q], parts[1][q]], axis=0) for q in range(WID)]
    else:
        quarters = split_rows(turned)
    put(place_ref, keep, send, base + spot[(wide, second, first)][0], [pack(q) for q in quarters])


def put_halves(place_ref, keep, send, spot, base, c, by_chosen, by_other):
    for b in range(WHOLE):
        put_half(place_ref, keep, send, spot, base, c, b, "tj", "tt", lanes(by_chosen, b))
        put_half(place_ref, keep, send, spot, base, c, b, "tt", "tj", lanes(by_other, b))
    put_half(place_ref, keep, send, spot, base, c, "p", "tj", "tt", lanes(by_chosen, WHOLE))
    if c > WHOLE:
        put_half(place_ref, keep, send, spot, base, c, "p", "tt", "tj", lanes(by_other, WHOLE))


def reorder_kernel(g_ref, *outs):
    tokens = g_ref.shape[1]
    half = g_ref.shape[0] // 2
    source = lax.broadcasted_iota(jnp.int32, (tokens, UNIT), 0)
    lane = lax.broadcasted_iota(jnp.int32, (tokens, UNIT), 1)

    def pick(wanted):
        return jnp.where(source == wanted, 1.0, 0.0).astype(jnp.bfloat16)

    for step in range(HALVES):
        for i, c in enumerate(STEPS[step]):
            wanted = (lane // SUB) * UNIT + c * SUB + lane % SUB
            chunk = dot(g_ref[...], pick(wanted), ((1,), (0,))).astype(jnp.bfloat16)
            outs[step][:, i * UNIT : (i + 1) * UNIT] = chunk
    size = SUB // 2
    for h in range(2):
        inner = lane % (UNIT // 2)
        wanted = (inner // size) * UNIT + WHOLE * SUB + h * size + inner % size
        upper = dot(g_ref[:half, :], pick(jnp.where(lane < UNIT // 2, wanted, -1)), ((1,), (0,)))
        lower = dot(g_ref[half:, :], pick(jnp.where(lane < UNIT // 2, -1, wanted)), ((1,), (0,)))
        outs[HALVES + h][...] = (upper + lower).astype(jnp.bfloat16)


def self_kernel(place_ref, a_ref, g_ref, keep, send):
    acts = a_ref[...]
    grads = g_ref[...]
    for i, block in enumerate((row_dot(acts, acts), dot(grads.T, grads, ((1,), (0,))))):
        for b in range(WID):
            put(place_ref, keep, send, (i * WID + b) * UNIT, split_rows(lanes(block, b)))


def acts_kernel(layouts, place_ref, own_ref, ring_ref, other_ref, keep, send):
    even = place_ref[0] == 0

    def arrival(x):
        spans = [(q * UNIT + c * SUB, SUB) for c in range(WHOLE) for q in range(WID)]
        spans += [(q * UNIT + WHOLE * SUB + h * (SUB // 2), SUB // 2) for h in range(2) for q in range(WID)]
        return jnp.concatenate([x[at : at + size] for at, size in spans], axis=0)

    own, ring, other = own_ref[...], ring_ref[...], other_ref[...]
    chosen = arrival(jnp.where(even, ring, own))
    ring = row_dot(arrival(ring), own)
    third = row_dot(chosen, arrival(other))
    base = 0
    for step, layout in enumerate(layouts):
        spot, ids = layout[0], STEPS[step]
        for c in ids:
            first = c * UNIT if c < WHOLE else WHOLE * UNIT + (c - WHOLE) * (UNIT // 2)
            rows = slice(first, first + (UNIT if c < WHOLE else UNIT // 2))
            put_ring(place_ref, keep, send, spot, base, c, ring[rows])
            if c < WHOLE:
                for b in range(ids[-1] + 1):
                    put_third(place_ref, keep, send, spot, base, c, b, lanes(third[rows], b))
                for a in range(ids[0]):
                    put_third(place_ref, keep, send, spot, base, a, c, lanes(third[a * UNIT : (a + 1) * UNIT], c))
            else:
                by_other = lanes(third, WHOLE).T[first - WHOLE * UNIT : first - WHOLE * UNIT + UNIT // 2]
                put_halves(place_ref, keep, send, spot, base, c, third[rows], by_other)
        base += layout[3]


PARTS = 4


def own_copies(own_hbm, own, sems):
    deep = own.shape[0] // PARTS
    spans = [pl.ds(k * deep, deep) for k in (0, 2, 1, 3)]
    return [pltpu.make_async_copy(own_hbm.at[at], own.at[at], sems.at[i]) for i, at in enumerate(spans)]


def grads_kernel(step, spot, place_ref, own_hbm, *refs):
    n = step + 1
    mine, ring, other, (keep, send, own, fresh, chosen, others, sems) = refs[:n], refs[n : 2 * n], refs[2 * n : 3 * n], refs[3 * n :]
    even = place_ref[0] == 0
    deep = own.shape[0] // PARTS
    ids = STEPS[step]
    before = ids[0] * UNIT

    def column(ref, a):
        return ref.at[:, STEPS[a][0] * UNIT : (STEPS[a][-1] + 1) * UNIT]

    first = pltpu.make_async_copy(ring[step], fresh, sems.at[PARTS])
    copies = own_copies(own_hbm, own, sems)
    third = [pltpu.make_async_copy(other[a], column(others, a), sems.at[PARTS + 1 + a]) for a in range(n)]
    from_ring = [pltpu.make_async_copy(ring[a], column(chosen, a), sems.at[PARTS + 1 + n + a]) for a in range(n)]
    from_mine = [pltpu.make_async_copy(mine[a], column(chosen, a), sems.at[PARTS + 1 + n + a]) for a in range(n)]
    first.start()
    for copy in copies:
        copy.start()

    @pl.when(even)
    def _():
        for copy in from_ring:
            copy.start()

    @pl.when(jnp.logical_not(even))
    def _():
        for copy in from_mine:
            copy.start()

    for copy in third:
        copy.start()
    first.wait()
    block = jnp.zeros((len(ids) * UNIT, own.shape[1]), jnp.float32)
    for copy, k in zip(copies, (0, 2, 1, 3)):
        copy.wait()
        at = pl.ds(k * deep, deep)
        block = block + dot(fresh[at, :].T, own[at, :], ((1,), (0,)))
    for i, c in enumerate(ids):
        put_ring(place_ref, keep, send, spot, 0, c, block[i * UNIT : (i + 1) * UNIT])
    for copy in from_ring + third:
        copy.wait()
    block = dot(column(chosen, step)[...].T, others[...], ((1,), (0,)))
    for i, c in enumerate(ids):
        for b in range(ids[-1] + 1):
            put_third(place_ref, keep, send, spot, 0, c, b, lanes(block[i * UNIT : (i + 1) * UNIT], b))
    if before:
        block = dot(column(others, step)[...].T, chosen[:, :before], ((1,), (0,))).T
        for a in range(ids[0]):
            for i, c in enumerate(ids):
                put_third(place_ref, keep, send, spot, 0, a, c, lanes(block[a * UNIT : (a + 1) * UNIT], i))


def halves_kernel(step, spot, place_ref, own_hbm, *refs):
    n = step - HALVES + 1
    count = step + 1
    c = STEPS[step][0]
    mine, ring, other, scratch = refs[:count], refs[count : 2 * count], refs[2 * count : 3 * count], refs[3 * count :]
    keep, send, own, fresh, chosen, others, chosen_part, other_part, sems = scratch
    even = place_ref[0] == 0
    deep = own.shape[0] // 2
    size = UNIT // 2

    def home(whole, part, a):
        return whole.at[:, STEPS[a][0] * UNIT : (STEPS[a][-1] + 1) * UNIT] if a < HALVES else part.at[a - HALVES]

    first = pltpu.make_async_copy(ring[step], fresh, sems.at[PARTS])
    copies = own_copies(own_hbm, own, sems)
    third = [pltpu.make_async_copy(other[a], home(others, other_part, a), sems.at[PARTS + 1 + a]) for a in range(count)]
    from_ring = [pltpu.make_async_copy(ring[a], home(chosen, chosen_part, a), sems.at[PARTS + 1 + count + a]) for a in range(count)]
    from_mine = [pltpu.make_async_copy(mine[a], home(chosen, chosen_part, a), sems.at[PARTS + 1 + count + a]) for a in range(count)]
    first.start()
    for copy in copies:
        copy.start()

    @pl.when(even)
    def _():
        for copy in from_ring:
            copy.start()

    @pl.when(jnp.logical_not(even))
    def _():
        for copy in from_mine:
            copy.start()

    for copy in third:
        copy.start()

    def against(turned, right):
        return dot(turned[:size], right[:deep, :], ((1,), (0,))) + dot(turned[size:], right[deep:, :], ((1,), (0,)))

    def against_half(turned, right):
        return dot(turned[:size], right, ((1,), (0,)))[:, :size] + dot(turned[size:], right, ((1,), (0,)))[:, size:]

    def product_of(turned, whole, part):
        halves = [against_half(turned, part[h]) for h in range(n)]
        return jnp.concatenate([against(turned, whole), halves[0], halves[-1]], axis=1)

    first.wait()
    part = own.shape[0] // PARTS
    block = jnp.zeros((size, own.shape[1]), jnp.float32)
    for i, copy in enumerate(copies):
        copy.wait()
        turned = fresh[(i // 2) * part : (i // 2 + 1) * part, :].T[(i % 2) * size : (i % 2 + 1) * size]
        k = (i % 2) * 2 + i // 2
        block = block + dot(turned, own[k * part : (k + 1) * part, :], ((1,), (0,)))
    put_ring(place_ref, keep, send, spot, 0, c, block)
    for copy in from_ring + third:
        copy.wait()
    by_chosen = product_of(chosen_part[n - 1].T, others, other_part)
    by_other = product_of(other_part[n - 1].T, chosen, chosen_part)
    put_halves(place_ref, keep, send, spot, 0, c, by_chosen, by_other)


def halves_scratch(own, step):
    deep, n = own.shape[0], step - HALVES + 1
    arrays = [pltpu.VMEM((deep, own.shape[1]), jnp.bfloat16), pltpu.VMEM((deep // 2, UNIT), jnp.bfloat16)]
    arrays += [pltpu.VMEM((deep, WHOLE * UNIT), jnp.bfloat16)] * 2 + [pltpu.VMEM((n, deep // 2, UNIT), jnp.bfloat16)] * 2
    return (*arrays, pltpu.SemaphoreType.DMA((PARTS + 1 + 2 * (step + 1),)))


def grads_scratch(own, step):
    deep, ids = own.shape[0], STEPS[step]
    widths = (own.shape[1], len(ids) * UNIT, (ids[-1] + 1) * UNIT, (ids[-1] + 1) * UNIT)
    arrays = [pltpu.VMEM((deep, width), jnp.bfloat16) for width in widths]
    return (*arrays, pltpu.SemaphoreType.DMA((PARTS + 1 + 2 * (step + 1),)))


def product(acts, grads, act_at, grad_at, rows):
    act_sum = acts[0][act_at : act_at + rows, :] + acts[1][act_at : act_at + rows, :]
    grad_sum = grads[0][grad_at : grad_at + rows, :] + grads[1][grad_at : grad_at + rows, :]
    return (act_sum * (1.0 / math.sqrt(D))) * (grad_sum * (1.0 / math.sqrt(FF)))


def return_kernel(layouts, steps, *refs):
    acts, (ring, swap) = refs[:2], refs[-2:]
    ring_at = swap_at = 0
    for i, c in enumerate(steps):
        grads = refs[2 + 2 * i : 4 + 2 * i]
        _, n_ring, n_swap, _ = layouts[c]
        base = sum(layouts[s][3] for s in range(c))
        ring[ring_at : ring_at + n_ring, :] = product(acts, grads, base, 0, n_ring)
        swap[swap_at : swap_at + n_swap - n_ring, :] = product(acts, grads, base + n_ring, n_ring, n_swap - n_ring)
        ring_at += n_ring
        swap_at += n_swap - n_ring


def last_kernel(base, first, *refs):
    acts, near, far, out = refs[:2], refs[2], refs[3], refs[4]
    n = out.shape[0]
    near_part = near.at[first : first + n, :]
    out[...] = product(acts, (near_part, far), base + first, 0, n)


def final_kernel(layouts, groups, place_ref, lengths_ref, *refs):
    last = len(layouts) - 1
    selves, acts, out = refs[:2], refs[2:4], refs[-1]
    grads = [refs[4 + 2 * c : 6 + 2 * c] for c in range(last)]
    near, far_ring, far_rest = refs[4 + 2 * last : 7 + 2 * last]
    rings, swaps = refs[7 + 2 * last : -1 : 2], refs[8 + 2 * last : -1 : 2]
    returned = {last: (rings[-1], 0, swaps[-1], -layouts[last][1])}
    for i, steps in enumerate(groups):
        ring_at = swap_at = 0
        for c in steps:
            _, n_ring, n_swap, _ = layouts[c]
            returned[c] = rings[i], ring_at, swaps[i], swap_at - n_ring
            ring_at += n_ring
            swap_at += n_swap - n_ring
    even = place_ref[0] == 0
    width = place_ref[3]
    token = place_ref[4]
    total = lengths_ref.shape[0]
    here = lengths_ref[token]
    columns = width * UNIT + lax.broadcasted_iota(jnp.int32, (UNIT, UNIT), 1)
    line = lax.broadcasted_iota(jnp.int32, (UNIT, UNIT), 0)

    step_of = {c: step for step, ids in enumerate(STEPS) for c in ids}

    def block(where, *name):
        step = step_of[max(x for x in name[1 : 2 if name[0] == "rj" else 3] if x != "p")]
        at, size = layouts[step][0][name]
        if where == "local":
            base = sum(layout[3] for layout in layouts[:step])
            if step < last:
                return product(acts, grads[step], base + at, at, size)
            n_ring = layouts[last][1]
            far, far_at = (far_ring, at) if at < n_ring else (far_rest, at - n_ring)
            return product(acts, (near.at[at : at + size, :], far.at[far_at : far_at + size, :]), base + at, 0, size)
        ring, ring_at, swap, swap_at = returned[step]
        ref, at = (ring, ring_at + at) if where == "ring" else (swap, swap_at + at)
        return ref[at : at + size, :]

    def beside(left, right):
        return jnp.concatenate([unpack(left), unpack(right)], axis=1)

    def third(where, kind, c):
        one, two = WHOLE, WHOLE + 1
        if c < WHOLE:
            rows = [block(where, kind, a, c) for a in (*range(WHOLE), one, two)]
        else:
            rows = [beside(block(where, kind, a, one), block(where, kind, a, two)) for a in range(WHOLE)]
            if kind == "tt":
                rows.append(beside(block(where, kind, "p", one), block(where, kind, "p", two))[: SUB // 2])
            else:
                crossed = unpack(block(where, kind, "p", two))[: SUB // 2]
                rows.append(jnp.concatenate([block(where, kind, one, "p")[:, : UNIT // 2], crossed], axis=1))
            rows.append(block(where, kind, two, "p"))
        return jnp.concatenate(rows, axis=0)

    def natural(offset, b, tile, there):
        live = (b * UNIT + line < here) & (columns < there)
        out[offset, b * UNIT : (b + 1) * UNIT, :] = jnp.where(live, tile.T, 0.0)

    def arrival(offset, c, tile, there):
        if c < WHOLE:
            token_at = (line // SUB) * UNIT + c * SUB + line % SUB
            spans = [(q * SUB, q * UNIT + c * SUB, SUB) for q in range(WID)]
        else:
            size = SUB // 2
            inner = line % (UNIT // 2)
            token_at = (inner // size) * UNIT + c * SUB + (line // (UNIT // 2)) * size + inner % size
            spans = [(h * (UNIT // 2) + q * size, q * UNIT + c * SUB + h * size, size) for h in range(2) for q in range(WID)]
        tile = jnp.where((token_at < here) & (columns < there), tile.T, 0.0)
        for at, first, size in spans:
            out[offset, first : first + size, :] = tile[at : at + size]

    there = [lengths_ref[lax.rem(token + offset + total - 2, total)] for offset in range(5)]
    for c in range(WHOLE + 1):
        rt = block("ring", "rt", c) if c < WHOLE else beside(block("ring", "rt", WHOLE), block("ring", "rt", WHOLE + 1))
        arrival(0, c, rt, there[0])
        arrival(1, c, jnp.where(even, third("ring", "tt", c), third("local", "tt", c)), there[1])
        arrival(3, c, third("swap", "tj", c), there[3])
    for b in range(WID):
        natural(2, b, product(selves, selves, b * UNIT, (WID + b) * UNIT, UNIT), there[2])
        natural(4, b, jnp.concatenate([block("local", "rj", c, b) for c in range(WHOLE + 2)], axis=0), there[4])


def shards(acts, grads, lengths):
    rows = acts.shape[0]
    length = lax.axis_size("tok")
    token = lax.axis_index("tok")
    width = lax.axis_index("wid")
    place = jnp.stack([token % 2, width % 2, width // 2, width, token]).astype(jnp.int32)
    swap = [(i, i ^ 1) for i in range(length)]
    down = [(i, (i - 2) % length) for i in range(length)]
    up = [(i, (i + 2) % length) for i in range(length)]
    layouts = step_layouts()

    def floats(n):
        return (jax.ShapeDtypeStruct((2, n, UNIT), jnp.float32),) * 2

    def over_core(send):
        return lax.ppermute(send, "wid", [(w, w ^ 1) for w in range(WID)])

    own_g = grads.T
    deep = grads.shape[1]
    shapes = [(deep, len(ids) * UNIT) if step < HALVES else (deep // 2, UNIT) for step, ids in enumerate(STEPS)]
    mine = call(reorder_kernel, tuple(jax.ShapeDtypeStruct(shape, jnp.bfloat16) for shape in shapes), own_g)
    alive = jnp.max(lengths) > 0
    seen = {}

    def after(x, names):
        if not names:
            return x
        x, *held = lax.optimization_barrier((x, *[seen[name] for name in names]))
        seen.update(zip(names, held))
        return x

    def start(name, chunk):
        seen["R" + name] = lax.ppermute(after(chunk, GATES.get("R" + name)), "tok", down)
        seen["O" + name] = lax.ppermute(after(chunk, GATES.get("O" + name)), "tok", swap)

    def exchange(name, kernel, n, first, *rest, cuts=(), **options):
        spans = list(zip((0, *cuts), (*cuts, n)))

        def summed(*args):
            keep, send = call(kernel, floats(n), place, *args, scalars=1, **options)
            arrived = over_core(send)
            return keep[0] + arrived[0], *[keep[1, a:b] + arrived[1, a:b] for a, b in spans]

        def nothing(*args):
            return tuple(jnp.zeros((b - a, UNIT), jnp.float32) for a, b in [(0, n)] + spans)

        first = after(first, GATES.get("K" + name))
        run = summed if name in PLAIN else lambda *args: lax.cond(alive, summed, nothing, *args)
        near, *far = run(first, *rest)
        for i, x in enumerate(far):
            label = "S" + name + "xy"[i : i + 1] * (len(far) > 1)
            seen[label] = lax.ppermute(after(x, GATES.get(label)), "wid", [(w, w ^ 2) for w in range(WID)])
        return near

    near = {}
    for piece in PIECES:
        if piece == "A":
            start(piece, acts)
        elif piece.isdigit():
            start(piece, mine[int(piece)])
        elif piece == "kS":
            near["S"] = exchange("S", self_kernel, 2 * WID * UNIT, acts, own_g)
        elif piece == "kA":
            everything = sum(size for _, _, _, size in layouts)
            near["A"] = exchange("A", lambda *refs: acts_kernel(layouts, *refs), everything, acts, seen["RA"], seen["OA"])
        else:
            c = int(piece[1])
            spot, size = layouts[c][0], layouts[c][3]
            kernel, scratch = grads_kernel, grads_scratch
            if c >= HALVES:
                kernel, scratch = halves_kernel, halves_scratch
            arrived = [seen["%s%d" % (side, a)] for side in "RO" for a in range(c + 1)]
            near[c] = seen["N%d" % c] = exchange(
                piece[1], lambda *refs, c=c, spot=spot, kernel=kernel: kernel(c, spot, *refs),
                size, own_g, *mine[: c + 1], *arrived, memory=pl.BlockSpec(memory_space=pl.ANY), scratch=scratch(own_g, c),
                cuts=(layouts[c][1],) if c + 1 == len(layouts) else (),
            )

    returned = []
    for i, steps in enumerate(GROUPS):
        sizes = [sum(layouts[c][1] for c in steps), sum(layouts[c][2] - layouts[c][1] for c in steps)]
        first = after(near[steps[0]], GATES.get("G%d" % i))
        grams = sum([[first if c == steps[0] else near[c], seen["S%d" % c]] for c in steps], [])
        ring, swapped = call(
            lambda *refs, steps=steps: return_kernel(layouts, steps, *refs),
            tuple(jax.ShapeDtypeStruct((n, UNIT), jnp.float32) for n in sizes),
            near["A"], seen["SA"], *grams,
        )
        returned += [lax.ppermute(ring, "tok", up), lax.ppermute(swapped, "tok", swap)]

    last = len(layouts) - 1
    base = sum(layout[3] for layout in layouts[:last])
    _, n_ring, n_swap, _ = layouts[last]
    for first, n, far, move in ((0, n_ring, "S%dx" % last, up), (n_ring, n_swap - n_ring, "S%dy" % last, swap)):
        tile = call(
            lambda *refs, first=first: last_kernel(base, first, *refs),
            jax.ShapeDtypeStruct((n, UNIT), jnp.float32), near["A"], seen["SA"], near[last], seen[far],
        )
        returned.append(lax.ppermute(tile, "tok", move))

    grams = sum([[near[c], seen["S%d" % c]] for c in range(last)], [near["A"], seen["SA"]])
    grams += [near[last], seen["S%dx" % last], seen["S%dy" % last]]
    out = call(
        lambda *refs: final_kernel(layouts, GROUPS, *refs),
        jax.ShapeDtypeStruct((5, rows, UNIT), jnp.float32),
        place, lengths, near["S"], seen["SS"], *grams, *returned, scalars=2,
    )
    return out.transpose(1, 0, 2)


def solution(mesh):
    return jax.shard_map(
        shards,
        mesh=mesh,
        in_specs=(P("tok", "wid"), P("tok", "wid"), P()),
        out_specs=P("tok", None, "wid"),
        check_vma=False,
    )
```

```python
import math

import jax
import jax.numpy as jnp
from jax import lax
from jax.experimental import pallas as pl
from jax.experimental.pallas import tpu as pltpu
from jax.sharding import PartitionSpec as P

D = 4096
FF = 11008
WID = 4
UNIT = 128
SUB = UNIT // WID
VMEM_LIMIT = 24 << 20
PIECES = ['A', '0', 'kS', '1', 'kA', '2', 'k0', '3', 'k1', 'g0', 'k2', 'g1', 'k3']
GATES = {'R1': ['RA'], 'O1': ['OA'], 'R2': ['RA'], 'O2': ['OA'], 'R3': ['R1'], 'O3': ['O1'], 'KA': [], 'K0': ['SS'], 'K1': ['SS'], 'K2': ['S0'], 'K3': ['V0'], 'SA': [], 'S0': [], 'S1': ['S0'], 'S2': [], 'S3x': [], 'S3y': ['V1'], 'G0': ['R2'], 'G1': []}
PLAIN = []
GROUPS = [[0, 1], [2]]
SMEM = pl.BlockSpec(memory_space=pltpu.SMEM)
VMEM = pl.BlockSpec(memory_space=pltpu.VMEM)


def call(kernel, outs, *args, scalars=0, memory=VMEM, scratch=()):
    return pl.pallas_call(
        kernel,
        out_shape=outs,
        in_specs=[SMEM] * scalars + [memory] * (len(args) - scalars),
        out_specs=jax.tree.map(lambda _: VMEM, outs),
        scratch_shapes=scratch,
        cost_estimate=pl.CostEstimate(flops=2000000000, bytes_accessed=2000000, transcendentals=0),
        compiler_params=pltpu.CompilerParams(vmem_limit_bytes=VMEM_LIMIT),
    )(*args)


def dot(left, right, dims):
    return lax.dot_general(left, right, (dims, ((), ())), preferred_element_type=jnp.float32)


def row_dot(left, right):
    return dot(left, right, ((1,), (1,)))


def put(place_ref, keep, send, at, quarters):
    core = place_ref[1] == 0
    side = place_ref[2] == 0
    rows = pl.ds(at, quarters[0].shape[0])
    kept = [jnp.where(core, quarters[2 * s], quarters[2 * s + 1]) for s in range(2)]
    sent = [jnp.where(core, quarters[2 * s + 1], quarters[2 * s]) for s in range(2)]
    for ref, pair in ((keep, kept), (send, sent)):
        ref[0, rows, :] = jnp.where(side, pair[0], pair[1])
        ref[1, rows, :] = jnp.where(side, pair[1], pair[0])


def split_rows(block):
    n = block.shape[0] // WID
    return [block[q * n : (q + 1) * n] for q in range(WID)]


def lanes(block, b):
    return block[:, b * UNIT : (b + 1) * UNIT]


def step_layout(step, units):
    fresh = [(step, b) for b in range(step + 1)] + [(a, step) for a in range(step)]
    at, spot = UNIT, {("rt", step): 0}
    for a, b in fresh:
        spot[("tt", b, a)] = at
        at += SUB
    n_ring = at
    for a, b in fresh:
        spot[("tj", a, b)] = at
        at += SUB
    n_swap = at
    for b in range(WID):
        spot[("rj", step, b)] = at
        at += SUB
    return spot, n_ring, n_swap, at


def put_ring(place_ref, keep, send, spot, base, step, block):
    columns = [lanes(block, b) for b in range(WID)]
    put(place_ref, keep, send, base + spot[("rt", step)], [c.T for c in columns])
    for b in range(WID):
        put(place_ref, keep, send, base + spot[("rj", step, b)], split_rows(columns[b]))


def put_third(place_ref, keep, send, spot, base, a, b, block):
    put(place_ref, keep, send, base + spot[("tj", a, b)], split_rows(block))
    put(place_ref, keep, send, base + spot[("tt", b, a)], split_rows(block.T))


def reorder_kernel(g_ref, *outs):
    units = len(outs)
    tokens = g_ref.shape[1]
    source = lax.broadcasted_iota(jnp.int32, (tokens, UNIT), 0)
    lane = lax.broadcasted_iota(jnp.int32, (tokens, UNIT), 1)
    for c, out in enumerate(outs):
        wanted = (lane // SUB) * UNIT + c * SUB + lane % SUB
        pick = jnp.where(source == wanted, 1.0, 0.0).astype(jnp.bfloat16)
        out[...] = dot(g_ref[...], pick, ((1,), (0,))).astype(jnp.bfloat16)


def self_kernel(place_ref, a_ref, g_ref, keep, send):
    acts = a_ref[...]
    grads = g_ref[...]
    for i, block in enumerate((row_dot(acts, acts), dot(grads.T, grads, ((1,), (0,))))):
        for b in range(WID):
            put(place_ref, keep, send, (i * WID + b) * UNIT, split_rows(lanes(block, b)))


def acts_kernel(layouts, place_ref, own_ref, ring_ref, other_ref, keep, send):
    units = len(layouts)
    even = place_ref[0] == 0

    def arrival(x):
        return jnp.concatenate([x[q * UNIT + c * SUB : q * UNIT + (c + 1) * SUB] for c in range(units) for q in range(WID)], axis=0)

    own, ring, other = own_ref[...], ring_ref[...], other_ref[...]
    chosen = arrival(jnp.where(even, ring, own))
    ring = arrival(ring)
    other = arrival(other)
    base = 0
    for c, (spot, _, _, size) in enumerate(layouts):
        put_ring(place_ref, keep, send, spot, base, c, row_dot(ring[c * UNIT : (c + 1) * UNIT], own))
        base += size
    for a in range(units):
        block = row_dot(chosen[a * UNIT : (a + 1) * UNIT], other)
        for b in range(units):
            step = max(a, b)
            base = sum(layouts[s][3] for s in range(step))
            put_third(place_ref, keep, send, layouts[step][0], base, a, b, lanes(block, b))


PARTS = 4


def own_copies(own_hbm, own, sems):
    deep = own.shape[0] // PARTS
    spans = [pl.ds(k * deep, deep) for k in (0, 2, 1, 3)]
    return [pltpu.make_async_copy(own_hbm.at[at], own.at[at], sems.at[i]) for i, at in enumerate(spans)]


def grads_kernel(step, spot, place_ref, own_hbm, *refs):
    n = step + 1
    mine, ring, other, (keep, send, own, fresh, chosen, others, sems) = refs[:n], refs[n : 2 * n], refs[2 * n : 3 * n], refs[3 * n :]
    even = place_ref[0] == 0
    deep = own.shape[0] // PARTS

    def column(ref, a):
        return ref.at[:, a * UNIT : (a + 1) * UNIT]

    first = pltpu.make_async_copy(ring[step], fresh, sems.at[PARTS])
    copies = own_copies(own_hbm, own, sems)
    third = [pltpu.make_async_copy(other[a], column(others, a), sems.at[PARTS + 1 + a]) for a in range(n)]
    from_ring = [pltpu.make_async_copy(ring[a], column(chosen, a), sems.at[PARTS + 1 + n + a]) for a in range(n)]
    from_mine = [pltpu.make_async_copy(mine[a], column(chosen, a), sems.at[PARTS + 1 + n + a]) for a in range(n)]
    first.start()
    for copy in copies:
        copy.start()

    @pl.when(even)
    def _():
        for copy in from_ring:
            copy.start()

    @pl.when(jnp.logical_not(even))
    def _():
        for copy in from_mine:
            copy.start()

    for copy in third:
        copy.start()
    first.wait()
    block = jnp.zeros((UNIT, own.shape[1]), jnp.float32)
    for copy, k in zip(copies, (0, 2, 1, 3)):
        copy.wait()
        at = pl.ds(k * deep, deep)
        block = block + dot(fresh[at, :].T, own[at, :], ((1,), (0,)))
    put_ring(place_ref, keep, send, spot, 0, step, block)
    for copy in from_ring + third:
        copy.wait()
    block = dot(column(chosen, step)[...].T, others[...], ((1,), (0,)))
    for b in range(n):
        put_third(place_ref, keep, send, spot, 0, step, b, lanes(block, b))
    if step:
        block = dot(column(others, step)[...].T, chosen[:, : step * UNIT], ((1,), (0,))).T
        for a in range(step):
            put_third(place_ref, keep, send, spot, 0, a, step, block[a * UNIT : (a + 1) * UNIT])


def grads_scratch(own, n):
    deep = own.shape[0]
    arrays = [pltpu.VMEM((deep, width), jnp.bfloat16) for width in (own.shape[1], UNIT, n * UNIT, n * UNIT)]
    return (*arrays, pltpu.SemaphoreType.DMA((PARTS + 1 + 2 * n,)))


def product(acts, grads, act_at, grad_at, rows):
    act_sum = acts[0][act_at : act_at + rows, :] + acts[1][act_at : act_at + rows, :]
    grad_sum = grads[0][grad_at : grad_at + rows, :] + grads[1][grad_at : grad_at + rows, :]
    return (act_sum * (1.0 / math.sqrt(D))) * (grad_sum * (1.0 / math.sqrt(FF)))


def return_kernel(layouts, steps, *refs):
    acts, (ring, swap) = refs[:2], refs[-2:]
    ring_at = swap_at = 0
    for i, c in enumerate(steps):
        grads = refs[2 + 2 * i : 4 + 2 * i]
        _, n_ring, n_swap, _ = layouts[c]
        base = sum(layouts[s][3] for s in range(c))
        ring[ring_at : ring_at + n_ring, :] = product(acts, grads, base, 0, n_ring)
        swap[swap_at : swap_at + n_swap - n_ring, :] = product(acts, grads, base + n_ring, n_ring, n_swap - n_ring)
        ring_at += n_ring
        swap_at += n_swap - n_ring


def last_kernel(base, first, *refs):
    acts, near, far, out = refs[:2], refs[2], refs[3], refs[4]
    n = out.shape[0]
    near_part = near.at[first : first + n, :]
    out[...] = product(acts, (near_part, far), base + first, 0, n)


def final_kernel(layouts, groups, place_ref, lengths_ref, *refs):
    units = len(layouts)
    last = units - 1
    selves, acts, out = refs[:2], refs[2:4], refs[-1]
    grads = [refs[4 + 2 * c : 6 + 2 * c] for c in range(last)]
    near, far_ring, far_rest = refs[4 + 2 * last : 7 + 2 * last]
    rings, swaps = refs[7 + 2 * last : -1 : 2], refs[8 + 2 * last : -1 : 2]
    returned = {last: (rings[-1], 0, swaps[-1], -layouts[last][1])}
    for i, steps in enumerate(groups):
        ring_at = swap_at = 0
        for c in steps:
            _, n_ring, n_swap, _ = layouts[c]
            returned[c] = rings[i], ring_at, swaps[i], swap_at - n_ring
            ring_at += n_ring
            swap_at += n_swap - n_ring
    even = place_ref[0] == 0
    width = place_ref[3]
    token = place_ref[4]
    total = lengths_ref.shape[0]
    here = lengths_ref[token]
    columns = width * UNIT + lax.broadcasted_iota(jnp.int32, (UNIT, UNIT), 1)
    line = lax.broadcasted_iota(jnp.int32, (UNIT, UNIT), 0)

    def block(where, name, step):
        spot = layouts[step][0][name]
        size = UNIT if name[0] == "rt" else SUB
        if where == "local":
            base = sum(layouts[s][3] for s in range(step))
            if step < last:
                return product(acts, grads[step], base + spot, spot, size)
            n_ring = layouts[last][1]
            far, at = (far_ring, spot) if spot < n_ring else (far_rest, spot - n_ring)
            return product(acts, (near.at[spot : spot + size, :], far.at[at : at + size, :]), base + spot, 0, size)
        ring, ring_at, swap, swap_at = returned[step]
        ref, at = (ring, ring_at + spot) if where == "ring" else (swap, swap_at + spot)
        return ref[at : at + size, :]

    def natural(offset, b, tile, there):
        live = (b * UNIT + line < here) & (columns < there)
        out[offset, b * UNIT : (b + 1) * UNIT, :] = jnp.where(live, tile.T, 0.0)

    def arrival(offset, c, tile, there):
        token_at = (line // SUB) * UNIT + c * SUB + line % SUB
        tile = jnp.where((token_at < here) & (columns < there), tile.T, 0.0)
        for q in range(WID):
            first = q * UNIT + c * SUB
            out[offset, first : first + SUB, :] = tile[q * SUB : (q + 1) * SUB]

    there = [lengths_ref[lax.rem(token + offset + total - 2, total)] for offset in range(5)]
    for c in range(units):
        arrival(0, c, block("ring", ("rt", c), c), there[0])
        tt = [jnp.concatenate([block(r, ("tt", a, c), max(a, c)) for a in range(units)], axis=0) for r in ("ring", "local")]
        arrival(1, c, jnp.where(even, tt[0], tt[1]), there[1])
        arrival(3, c, jnp.concatenate([block("swap", ("tj", a, c), max(a, c)) for a in range(units)], axis=0), there[3])
    for b in range(WID):
        natural(2, b, product(selves, selves, b * UNIT, (WID + b) * UNIT, UNIT), there[2])
        natural(4, b, jnp.concatenate([block("local", ("rj", c, b), c) for c in range(units)], axis=0), there[4])


def shards(acts, grads, lengths):
    rows = acts.shape[0]
    units = rows // UNIT
    length = lax.axis_size("tok")
    token = lax.axis_index("tok")
    width = lax.axis_index("wid")
    place = jnp.stack([token % 2, width % 2, width // 2, width, token]).astype(jnp.int32)
    swap = [(i, i ^ 1) for i in range(length)]
    down = [(i, (i - 2) % length) for i in range(length)]
    up = [(i, (i + 2) % length) for i in range(length)]
    layouts = [step_layout(c, units) for c in range(units)]

    def floats(n):
        return (jax.ShapeDtypeStruct((2, n, UNIT), jnp.float32),) * 2

    def over_core(send):
        return lax.ppermute(send, "wid", [(w, w ^ 1) for w in range(WID)])

    own_g = grads.T
    mine = list(call(reorder_kernel, (jax.ShapeDtypeStruct((grads.shape[1], UNIT), jnp.bfloat16),) * units, own_g))
    alive = jnp.max(lengths) > 0
    seen = {}

    def after(x, names):
        if not names:
            return x
        x, *held = lax.optimization_barrier((x, *[seen[name] for name in names]))
        seen.update(zip(names, held))
        return x

    def start(name, chunk):
        seen["R" + name] = lax.ppermute(after(chunk, GATES.get("R" + name)), "tok", down)
        seen["O" + name] = lax.ppermute(after(chunk, GATES.get("O" + name)), "tok", swap)

    def exchange(name, kernel, n, first, *rest, cuts=(), **options):
        spans = list(zip((0, *cuts), (*cuts, n)))

        def summed(*args):
            keep, send = call(kernel, floats(n), place, *args, scalars=1, **options)
            arrived = over_core(send)
            return keep[0] + arrived[0], *[keep[1, a:b] + arrived[1, a:b] for a, b in spans]

        def nothing(*args):
            return tuple(jnp.zeros((b - a, UNIT), jnp.float32) for a, b in [(0, n)] + spans)

        first = after(first, GATES.get("K" + name))
        run = summed if name in PLAIN else lambda *args: lax.cond(alive, summed, nothing, *args)
        near, *far = run(first, *rest)
        for i, x in enumerate(far):
            label = "S" + name + "xy"[i : i + 1] * (len(far) > 1)
            seen[label] = lax.ppermute(after(x, GATES.get(label)), "wid", [(w, w ^ 2) for w in range(WID)])
        return near

    def pair(c):
        if str(c) in PIECES:
            return seen["R%d" % c], seen["O%d" % c]
        return tuple(jnp.concatenate([seen["%s%d%s" % (side, c, half)] for half in "ab"], axis=0) for side in "RO")

    near = {}

    def send_back(i, steps):
        sizes = [sum(layouts[c][1] for c in steps), sum(layouts[c][2] - layouts[c][1] for c in steps)]
        first = after(near[steps[0]], GATES.get("G%d" % i))
        grams = sum([[first if c == steps[0] else near[c], seen["S%d" % c]] for c in steps], [])
        ring, swapped = call(
            lambda *refs: return_kernel(layouts, steps, *refs),
            tuple(jax.ShapeDtypeStruct((n, UNIT), jnp.float32) for n in sizes),
            near["A"], seen["SA"], *grams,
        )
        seen["V%d" % i] = ring
        seen["U%d" % i] = lax.ppermute(ring, "tok", up)
        seen["X%d" % i] = lax.ppermute(swapped, "tok", swap)

    for piece in PIECES:
        if piece == "A":
            start(piece, acts)
        elif piece[0] in "0123":
            chunk = mine[int(piece[0])]
            cut = chunk.shape[0] // 2
            start(piece, {"": chunk, "a": chunk[:cut], "b": chunk[cut:]}[piece[1:]])
        elif piece[0] == "g":
            send_back(int(piece[1:]), GROUPS[int(piece[1:])])
        elif piece == "kS":
            near["S"] = exchange("S", self_kernel, 2 * WID * UNIT, acts, own_g)
        elif piece == "kA":
            everything = sum(size for _, _, _, size in layouts)
            near["A"] = exchange("A", lambda *refs: acts_kernel(layouts, *refs), everything, acts, seen["RA"], seen["OA"])
        else:
            c = int(piece[1])
            spot, size = layouts[c][0], layouts[c][3]
            pairs = [pair(a) for a in range(c + 1)]
            near[c] = seen["N%d" % c] = exchange(
                piece[1], lambda *refs, c=c, spot=spot: grads_kernel(c, spot, *refs),
                size, own_g, *mine[: c + 1], *[p[0] for p in pairs], *[p[1] for p in pairs],
                memory=pl.BlockSpec(memory_space=pl.ANY), scratch=grads_scratch(own_g, c + 1),
                cuts=(layouts[c][1],) if c + 1 == units else (),
            )

    returned = []
    for i in range(len(GROUPS)):
        returned += [seen["U%d" % i], seen["X%d" % i]]

    last = units - 1
    base = sum(layout[3] for layout in layouts[:last])
    _, n_ring, n_swap, _ = layouts[last]
    for first, n, far, move in ((0, n_ring, "S%dx" % last, up), (n_ring, n_swap - n_ring, "S%dy" % last, swap)):
        tile = call(
            lambda *refs, first=first: last_kernel(base, first, *refs),
            jax.ShapeDtypeStruct((n, UNIT), jnp.float32), near["A"], seen["SA"], near[last], seen[far],
        )
        returned.append(lax.ppermute(tile, "tok", move))

    grams = sum([[near[c], seen["S%d" % c]] for c in range(last)], [near["A"], seen["SA"]])
    grams += [near[last], seen["S%dx" % last], seen["S%dy" % last]]
    out = call(
        lambda *refs: final_kernel(layouts, GROUPS, *refs),
        jax.ShapeDtypeStruct((5, rows, UNIT), jnp.float32),
        place, lengths, near["S"], seen["SS"], *grams, *returned, scalars=2,
    )
    return out.transpose(1, 0, 2)


def solution(mesh):
    return jax.shard_map(
        shards,
        mesh=mesh,
        in_specs=(P("tok", "wid"), P("tok", "wid"), P()),
        out_specs=P("tok", None, "wid"),
        check_vma=False,
    )
```

```python
import math

import jax
import jax.numpy as jnp
from jax import lax
from jax.experimental import pallas as pl
from jax.experimental.pallas import tpu as pltpu
from jax.sharding import PartitionSpec as P

D = 4096
FF = 11008
WID = 4
UNIT = 128
SUB = UNIT // WID
VMEM_LIMIT = 24 << 20
PIECES = ['A', '0', 'kS', '1', 'kA', '2', 'k0', '3', 'k1', 'g0', 'k2', 'g1', 'k3']
GATES = {'R1': ['RA'], 'O1': ['OA'], 'R2': ['RA'], 'O2': ['OA'], 'R3': ['R0'], 'O3': ['O0'], 'KA': [], 'K0': ['SS'], 'K1': ['SS'], 'K2': ['S0'], 'K3': ['V0'], 'SA': [], 'S0': [], 'S1': ['S0'], 'S2': ['S1'], 'S3x': [], 'S3y': [], 'S3z': ['S3x'], 'G0': [], 'G1': []}
PLAIN = []
GROUPS = [[0, 1], [2]]
SMEM = pl.BlockSpec(memory_space=pltpu.SMEM)
VMEM = pl.BlockSpec(memory_space=pltpu.VMEM)


def call(kernel, outs, *args, scalars=0, memory=VMEM, scratch=()):
    return pl.pallas_call(
        kernel,
        out_shape=outs,
        in_specs=[SMEM] * scalars + [memory] * (len(args) - scalars),
        out_specs=jax.tree.map(lambda _: VMEM, outs),
        scratch_shapes=scratch,
        cost_estimate=pl.CostEstimate(flops=2000000000, bytes_accessed=2000000, transcendentals=0),
        compiler_params=pltpu.CompilerParams(vmem_limit_bytes=VMEM_LIMIT),
    )(*args)


def dot(left, right, dims):
    return lax.dot_general(left, right, (dims, ((), ())), preferred_element_type=jnp.float32)


def row_dot(left, right):
    return dot(left, right, ((1,), (1,)))


def put(place_ref, keep, send, at, quarters):
    core = place_ref[1] == 0
    side = place_ref[2] == 0
    rows = pl.ds(at, quarters[0].shape[0])
    kept = [jnp.where(core, quarters[2 * s], quarters[2 * s + 1]) for s in range(2)]
    sent = [jnp.where(core, quarters[2 * s + 1], quarters[2 * s]) for s in range(2)]
    for ref, pair in ((keep, kept), (send, sent)):
        ref[0, rows, :] = jnp.where(side, pair[0], pair[1])
        ref[1, rows, :] = jnp.where(side, pair[1], pair[0])


def split_rows(block):
    n = block.shape[0] // WID
    return [block[q * n : (q + 1) * n] for q in range(WID)]


def lanes(block, b):
    return block[:, b * UNIT : (b + 1) * UNIT]


def step_layout(step, units):
    fresh = [(step, b) for b in range(step + 1)] + [(a, step) for a in range(step)]
    at, spot = UNIT, {("rt", step): 0}
    for a, b in fresh:
        spot[("tt", b, a)] = at
        at += SUB
    n_ring = at
    for a, b in fresh:
        spot[("tj", a, b)] = at
        at += SUB
    n_swap = at
    for b in range(WID):
        spot[("rj", step, b)] = at
        at += SUB
    return spot, n_ring, n_swap, at


def put_ring(place_ref, keep, send, spot, base, step, block):
    columns = [lanes(block, b) for b in range(WID)]
    put(place_ref, keep, send, base + spot[("rt", step)], [c.T for c in columns])
    for b in range(WID):
        put(place_ref, keep, send, base + spot[("rj", step, b)], split_rows(columns[b]))


def put_third(place_ref, keep, send, spot, base, a, b, block):
    put(place_ref, keep, send, base + spot[("tj", a, b)], split_rows(block))
    put(place_ref, keep, send, base + spot[("tt", b, a)], split_rows(block.T))


def reorder_kernel(g_ref, *outs):
    units = len(outs)
    tokens = g_ref.shape[1]
    source = lax.broadcasted_iota(jnp.int32, (tokens, UNIT), 0)
    lane = lax.broadcasted_iota(jnp.int32, (tokens, UNIT), 1)
    for c, out in enumerate(outs):
        wanted = (lane // SUB) * UNIT + c * SUB + lane % SUB
        pick = jnp.where(source == wanted, 1.0, 0.0).astype(jnp.bfloat16)
        out[...] = dot(g_ref[...], pick, ((1,), (0,))).astype(jnp.bfloat16)


def self_kernel(place_ref, a_ref, g_ref, keep, send):
    acts = a_ref[...]
    grads = g_ref[...]
    for i, block in enumerate((row_dot(acts, acts), dot(grads.T, grads, ((1,), (0,))))):
        for b in range(WID):
            put(place_ref, keep, send, (i * WID + b) * UNIT, split_rows(lanes(block, b)))


def acts_kernel(layouts, place_ref, own_ref, ring_ref, other_ref, keep, send):
    units = len(layouts)
    even = place_ref[0] == 0

    def arrival(x):
        return jnp.concatenate([x[q * UNIT + c * SUB : q * UNIT + (c + 1) * SUB] for c in range(units) for q in range(WID)], axis=0)

    own, ring, other = own_ref[...], ring_ref[...], other_ref[...]
    chosen = arrival(jnp.where(even, ring, own))
    ring = arrival(ring)
    other = arrival(other)
    base = 0
    for c, (spot, _, _, size) in enumerate(layouts):
        put_ring(place_ref, keep, send, spot, base, c, row_dot(ring[c * UNIT : (c + 1) * UNIT], own))
        base += size
    for a in range(units):
        block = row_dot(chosen[a * UNIT : (a + 1) * UNIT], other)
        for b in range(units):
            step = max(a, b)
            base = sum(layouts[s][3] for s in range(step))
            put_third(place_ref, keep, send, layouts[step][0], base, a, b, lanes(block, b))


PARTS = 4


def own_copies(own_hbm, own, sems):
    deep = own.shape[0] // PARTS
    spans = [pl.ds(k * deep, deep) for k in (0, 2, 1, 3)]
    return [pltpu.make_async_copy(own_hbm.at[at], own.at[at], sems.at[i]) for i, at in enumerate(spans)]


def grads_kernel(step, spot, place_ref, own_hbm, *refs):
    n = step + 1
    mine, ring, other, (keep, send, own, fresh, chosen, others, sems) = refs[:n], refs[n : 2 * n], refs[2 * n : 3 * n], refs[3 * n :]
    even = place_ref[0] == 0
    deep = own.shape[0] // PARTS

    def column(ref, a):
        return ref.at[:, a * UNIT : (a + 1) * UNIT]

    first = pltpu.make_async_copy(ring[step], fresh, sems.at[PARTS])
    copies = own_copies(own_hbm, own, sems)
    third = [pltpu.make_async_copy(other[a], column(others, a), sems.at[PARTS + 1 + a]) for a in range(n)]
    from_ring = [pltpu.make_async_copy(ring[a], column(chosen, a), sems.at[PARTS + 1 + n + a]) for a in range(n)]
    from_mine = [pltpu.make_async_copy(mine[a], column(chosen, a), sems.at[PARTS + 1 + n + a]) for a in range(n)]
    first.start()
    for copy in copies:
        copy.start()

    @pl.when(even)
    def _():
        for copy in from_ring:
            copy.start()

    @pl.when(jnp.logical_not(even))
    def _():
        for copy in from_mine:
            copy.start()

    for copy in third:
        copy.start()
    first.wait()
    block = jnp.zeros((UNIT, own.shape[1]), jnp.float32)
    for copy, k in zip(copies, (0, 2, 1, 3)):
        copy.wait()
        at = pl.ds(k * deep, deep)
        block = block + dot(fresh[at, :].T, own[at, :], ((1,), (0,)))
    put_ring(place_ref, keep, send, spot, 0, step, block)
    for copy in from_ring + third:
        copy.wait()
    block = dot(column(chosen, step)[...].T, others[...], ((1,), (0,)))
    for b in range(n):
        put_third(place_ref, keep, send, spot, 0, step, b, lanes(block, b))
    if step:
        block = dot(column(others, step)[...].T, chosen[:, : step * UNIT], ((1,), (0,))).T
        for a in range(step):
            put_third(place_ref, keep, send, spot, 0, a, step, block[a * UNIT : (a + 1) * UNIT])


def grads_scratch(own, n):
    deep = own.shape[0]
    arrays = [pltpu.VMEM((deep, width), jnp.bfloat16) for width in (own.shape[1], UNIT, n * UNIT, n * UNIT)]
    return (*arrays, pltpu.SemaphoreType.DMA((PARTS + 1 + 2 * n,)))


def product(acts, grads, act_at, grad_at, rows):
    act_sum = acts[0][act_at : act_at + rows, :] + acts[1][act_at : act_at + rows, :]
    grad_sum = grads[0][grad_at : grad_at + rows, :] + grads[1][grad_at : grad_at + rows, :]
    return (act_sum * (1.0 / math.sqrt(D))) * (grad_sum * (1.0 / math.sqrt(FF)))


def return_kernel(layouts, steps, *refs):
    acts, (ring, swap) = refs[:2], refs[-2:]
    ring_at = swap_at = 0
    for i, c in enumerate(steps):
        grads = refs[2 + 2 * i : 4 + 2 * i]
        _, n_ring, n_swap, _ = layouts[c]
        base = sum(layouts[s][3] for s in range(c))
        ring[ring_at : ring_at + n_ring, :] = product(acts, grads, base, 0, n_ring)
        swap[swap_at : swap_at + n_swap - n_ring, :] = product(acts, grads, base + n_ring, n_ring, n_swap - n_ring)
        ring_at += n_ring
        swap_at += n_swap - n_ring


def last_kernel(base, first, *refs):
    acts, near, far, out = refs[:2], refs[2], refs[3], refs[4]
    n = out.shape[0]
    near_part = near.at[first : first + n, :]
    out[...] = product(acts, (near_part, far), base + first, 0, n)


def final_kernel(layouts, groups, place_ref, lengths_ref, *refs):
    units = len(layouts)
    last = units - 1
    selves, acts, out = refs[:2], refs[2:4], refs[-1]
    grads = [refs[4 + 2 * c : 6 + 2 * c] for c in range(last)]
    near, far_ring, far_rest = refs[4 + 2 * last : 7 + 2 * last]
    rings, swaps = refs[7 + 2 * last : -1 : 2], refs[8 + 2 * last : -1 : 2]
    returned = {last: (rings[-1], 0, swaps[-1], -layouts[last][1])}
    for i, steps in enumerate(groups):
        ring_at = swap_at = 0
        for c in steps:
            _, n_ring, n_swap, _ = layouts[c]
            returned[c] = rings[i], ring_at, swaps[i], swap_at - n_ring
            ring_at += n_ring
            swap_at += n_swap - n_ring
    even = place_ref[0] == 0
    width = place_ref[3]
    token = place_ref[4]
    total = lengths_ref.shape[0]
    here = lengths_ref[token]
    columns = width * UNIT + lax.broadcasted_iota(jnp.int32, (UNIT, UNIT), 1)
    line = lax.broadcasted_iota(jnp.int32, (UNIT, UNIT), 0)

    def block(where, name, step):
        spot = layouts[step][0][name]
        size = UNIT if name[0] == "rt" else SUB
        if where == "local":
            base = sum(layouts[s][3] for s in range(step))
            if step < last:
                return product(acts, grads[step], base + spot, spot, size)
            _, n_ring, n_swap, _ = layouts[last]
            far, at = (far_ring, spot) if spot < n_ring else (far_rest, spot - n_swap)
            return product(acts, (near.at[spot : spot + size, :], far.at[at : at + size, :]), base + spot, 0, size)
        ring, ring_at, swap, swap_at = returned[step]
        ref, at = (ring, ring_at + spot) if where == "ring" else (swap, swap_at + spot)
        return ref[at : at + size, :]

    def natural(offset, b, tile, there):
        live = (b * UNIT + line < here) & (columns < there)
        out[offset, b * UNIT : (b + 1) * UNIT, :] = jnp.where(live, tile.T, 0.0)

    def arrival(offset, c, tile, there):
        token_at = (line // SUB) * UNIT + c * SUB + line % SUB
        tile = jnp.where((token_at < here) & (columns < there), tile.T, 0.0)
        for q in range(WID):
            first = q * UNIT + c * SUB
            out[offset, first : first + SUB, :] = tile[q * SUB : (q + 1) * SUB]

    there = [lengths_ref[lax.rem(token + offset + total - 2, total)] for offset in range(5)]
    for c in range(units):
        arrival(0, c, block("ring", ("rt", c), c), there[0])
        tt = [jnp.concatenate([block(r, ("tt", a, c), max(a, c)) for a in range(units)], axis=0) for r in ("ring", "local")]
        arrival(1, c, jnp.where(even, tt[0], tt[1]), there[1])
        arrival(3, c, jnp.concatenate([block("swap", ("tj", a, c), max(a, c)) for a in range(units)], axis=0), there[3])
    for b in range(WID):
        natural(2, b, product(selves, selves, b * UNIT, (WID + b) * UNIT, UNIT), there[2])
        natural(4, b, jnp.concatenate([block("local", ("rj", c, b), c) for c in range(units)], axis=0), there[4])


def shards(acts, grads, lengths):
    rows = acts.shape[0]
    units = rows // UNIT
    length = lax.axis_size("tok")
    token = lax.axis_index("tok")
    width = lax.axis_index("wid")
    place = jnp.stack([token % 2, width % 2, width // 2, width, token]).astype(jnp.int32)
    swap = [(i, i ^ 1) for i in range(length)]
    down = [(i, (i - 2) % length) for i in range(length)]
    up = [(i, (i + 2) % length) for i in range(length)]
    layouts = [step_layout(c, units) for c in range(units)]

    def floats(n):
        return (jax.ShapeDtypeStruct((2, n, UNIT), jnp.float32),) * 2

    def over_core(send):
        return lax.ppermute(send, "wid", [(w, w ^ 1) for w in range(WID)])

    own_g = grads.T
    mine = list(call(reorder_kernel, (jax.ShapeDtypeStruct((grads.shape[1], UNIT), jnp.bfloat16),) * units, own_g))
    alive = jnp.max(lengths) > 0
    seen = {}

    def after(x, names):
        if not names:
            return x
        x, *held = lax.optimization_barrier((x, *[seen[name] for name in names]))
        seen.update(zip(names, held))
        return x

    def start(name, chunk):
        seen["R" + name] = lax.ppermute(after(chunk, GATES.get("R" + name)), "tok", down)
        seen["O" + name] = lax.ppermute(after(chunk, GATES.get("O" + name)), "tok", swap)

    def exchange(name, kernel, n, first, *rest, cuts=(), **options):
        spans = list(zip((0, *cuts), (*cuts, n)))

        def summed(*args):
            keep, send = call(kernel, floats(n), place, *args, scalars=1, **options)
            arrived = over_core(send)
            return keep[0] + arrived[0], *[keep[1, a:b] + arrived[1, a:b] for a, b in spans]

        def nothing(*args):
            return tuple(jnp.zeros((b - a, UNIT), jnp.float32) for a, b in [(0, n)] + spans)

        first = after(first, GATES.get("K" + name))
        run = summed if name in PLAIN else lambda *args: lax.cond(alive, summed, nothing, *args)
        near, *far = run(first, *rest)
        for i, x in enumerate(far):
            label = "S" + name + "xyz"[i : i + 1] * (len(far) > 1)
            seen[label] = lax.ppermute(after(x, GATES.get(label)), "wid", [(w, w ^ 2) for w in range(WID)])
        return near

    def pair(c):
        if str(c) in PIECES:
            return seen["R%d" % c], seen["O%d" % c]
        return tuple(jnp.concatenate([seen["%s%d%s" % (side, c, half)] for half in "ab"], axis=0) for side in "RO")

    near = {}

    def send_back(i, steps):
        sizes = [sum(layouts[c][1] for c in steps), sum(layouts[c][2] - layouts[c][1] for c in steps)]
        first = after(near[steps[0]], GATES.get("G%d" % i))
        grams = sum([[first if c == steps[0] else near[c], seen["S%d" % c]] for c in steps], [])
        ring, swapped = call(
            lambda *refs: return_kernel(layouts, steps, *refs),
            tuple(jax.ShapeDtypeStruct((n, UNIT), jnp.float32) for n in sizes),
            near["A"], seen["SA"], *grams,
        )
        seen["V%d" % i] = ring
        seen["U%d" % i] = lax.ppermute(ring, "tok", up)
        seen["X%d" % i] = lax.ppermute(swapped, "tok", swap)

    for piece in PIECES:
        if piece == "A":
            start(piece, acts)
        elif piece[0] in "0123":
            chunk = mine[int(piece[0])]
            cut = chunk.shape[0] // 2
            start(piece, {"": chunk, "a": chunk[:cut], "b": chunk[cut:]}[piece[1:]])
        elif piece[0] == "g":
            send_back(int(piece[1:]), GROUPS[int(piece[1:])])
        elif piece == "kS":
            near["S"] = exchange("S", self_kernel, 2 * WID * UNIT, acts, own_g)
        elif piece == "kA":
            everything = sum(size for _, _, _, size in layouts)
            near["A"] = exchange("A", lambda *refs: acts_kernel(layouts, *refs), everything, acts, seen["RA"], seen["OA"])
        else:
            c = int(piece[1])
            spot, size = layouts[c][0], layouts[c][3]
            pairs = [pair(a) for a in range(c + 1)]
            near[c] = seen["N%d" % c] = exchange(
                piece[1], lambda *refs, c=c, spot=spot: grads_kernel(c, spot, *refs),
                size, own_g, *mine[: c + 1], *[p[0] for p in pairs], *[p[1] for p in pairs],
                memory=pl.BlockSpec(memory_space=pl.ANY), scratch=grads_scratch(own_g, c + 1),
                cuts=layouts[c][1:3] if c + 1 == units else (),
            )

    returned = []
    for i in range(len(GROUPS)):
        returned += [seen["U%d" % i], seen["X%d" % i]]

    last = units - 1
    base = sum(layout[3] for layout in layouts[:last])
    _, n_ring, n_swap, _ = layouts[last]
    for first, n, far, move in ((0, n_ring, "S%dx" % last, up), (n_ring, n_swap - n_ring, "S%dy" % last, swap)):
        tile = call(
            lambda *refs, first=first: last_kernel(base, first, *refs),
            jax.ShapeDtypeStruct((n, UNIT), jnp.float32), near["A"], seen["SA"], near[last], seen[far],
        )
        returned.append(lax.ppermute(tile, "tok", move))

    grams = sum([[near[c], seen["S%d" % c]] for c in range(last)], [near["A"], seen["SA"]])
    grams += [near[last], seen["S%dx" % last], seen["S%dz" % last]]
    out = call(
        lambda *refs: final_kernel(layouts, GROUPS, *refs),
        jax.ShapeDtypeStruct((5, rows, UNIT), jnp.float32),
        place, lengths, near["S"], seen["SS"], *grams, *returned, scalars=2,
    )
    return out.transpose(1, 0, 2)


def solution(mesh):
    return jax.shard_map(
        shards,
        mesh=mesh,
        in_specs=(P("tok", "wid"), P("tok", "wid"), P()),
        out_specs=P("tok", None, "wid"),
        check_vma=False,
    )
```

```python
import math

import jax
import jax.numpy as jnp
from jax import lax
from jax.experimental import pallas as pl
from jax.experimental.pallas import tpu as pltpu
from jax.sharding import PartitionSpec as P

D = 4096
FF = 11008
WID = 4
UNIT = 128
SUB = UNIT // WID
VMEM_LIMIT = 24 << 20
PIECES = ['A', '0', 'kS', '1', 'kA', '2', 'k0', '3', 'k1', 'g0', 'k2', 'g1', 'k3']
GATES = {'R1': ['RA'], 'O1': ['OA'], 'R2': ['RA'], 'O2': ['OA'], 'R3': ['R0'], 'O3': ['O0'], 'KA': [], 'K0': ['SS'], 'K1': ['SS'], 'K2': ['S0'], 'K3': ['V0'], 'SA': [], 'S0': [], 'S1': ['S0'], 'S2': ['S1'], 'S3x': [], 'S3y': [], 'S3z': ['S3x'], 'G0': [], 'G1': []}
PLAIN = []
GROUPS = [[0, 1], [2]]
SMEM = pl.BlockSpec(memory_space=pltpu.SMEM)
VMEM = pl.BlockSpec(memory_space=pltpu.VMEM)


def call(kernel, outs, *args, scalars=0, memory=VMEM, scratch=()):
    return pl.pallas_call(
        kernel,
        out_shape=outs,
        in_specs=[SMEM] * scalars + [memory] * (len(args) - scalars),
        out_specs=jax.tree.map(lambda _: VMEM, outs),
        scratch_shapes=scratch,
        cost_estimate=pl.CostEstimate(flops=2000000000, bytes_accessed=2000000, transcendentals=0),
        compiler_params=pltpu.CompilerParams(vmem_limit_bytes=VMEM_LIMIT),
    )(*args)


def dot(left, right, dims):
    return lax.dot_general(left, right, (dims, ((), ())), preferred_element_type=jnp.float32)


def row_dot(left, right):
    return dot(left, right, ((1,), (1,)))


def put(place_ref, keep, send, at, quarters):
    core = place_ref[1] == 0
    side = place_ref[2] == 0
    rows = pl.ds(at, quarters[0].shape[0])
    kept = [jnp.where(core, quarters[2 * s], quarters[2 * s + 1]) for s in range(2)]
    sent = [jnp.where(core, quarters[2 * s + 1], quarters[2 * s]) for s in range(2)]
    for ref, pair in ((keep, kept), (send, sent)):
        ref[0, rows, :] = jnp.where(side, pair[0], pair[1])
        ref[1, rows, :] = jnp.where(side, pair[1], pair[0])


def split_rows(block):
    n = block.shape[0] // WID
    return [block[q * n : (q + 1) * n] for q in range(WID)]


def lanes(block, b):
    return block[:, b * UNIT : (b + 1) * UNIT]


def step_layout(step, units):
    fresh = [(step, b) for b in range(step + 1)] + [(a, step) for a in range(step)]
    at, spot = UNIT, {("rt", step): 0}
    for a, b in fresh:
        spot[("tt", b, a)] = at
        at += SUB
    n_ring = at
    for a, b in fresh:
        spot[("tj", a, b)] = at
        at += SUB
    n_swap = at
    for b in range(WID):
        spot[("rj", step, b)] = at
        at += SUB
    return spot, n_ring, n_swap, at


def put_ring(place_ref, keep, send, spot, base, step, block):
    columns = [lanes(block, b) for b in range(WID)]
    put(place_ref, keep, send, base + spot[("rt", step)], [c.T for c in columns])
    for b in range(WID):
        put(place_ref, keep, send, base + spot[("rj", step, b)], split_rows(columns[b]))


def put_third(place_ref, keep, send, spot, base, a, b, block):
    put(place_ref, keep, send, base + spot[("tj", a, b)], split_rows(block))
    put(place_ref, keep, send, base + spot[("tt", b, a)], split_rows(block.T))


def reorder_kernel(g_ref, *outs):
    units = len(outs)
    tokens = g_ref.shape[1]
    source = lax.broadcasted_iota(jnp.int32, (tokens, UNIT), 0)
    lane = lax.broadcasted_iota(jnp.int32, (tokens, UNIT), 1)
    for c, out in enumerate(outs):
        wanted = (lane // SUB) * UNIT + c * SUB + lane % SUB
        pick = jnp.where(source == wanted, 1.0, 0.0).astype(jnp.bfloat16)
        out[...] = dot(g_ref[...], pick, ((1,), (0,))).astype(jnp.bfloat16)


def self_kernel(place_ref, a_ref, g_ref, keep, send):
    acts = a_ref[...]
    grads = g_ref[...]
    for i, block in enumerate((row_dot(acts, acts), dot(grads.T, grads, ((1,), (0,))))):
        for b in range(WID):
            put(place_ref, keep, send, (i * WID + b) * UNIT, split_rows(lanes(block, b)))


def acts_kernel(layouts, place_ref, own_ref, ring_ref, other_ref, keep, send):
    units = len(layouts)
    even = place_ref[0] == 0

    def arrival(x):
        return jnp.concatenate([x[q * UNIT + c * SUB : q * UNIT + (c + 1) * SUB] for c in range(units) for q in range(WID)], axis=0)

    own, ring, other = own_ref[...], ring_ref[...], other_ref[...]
    chosen = arrival(jnp.where(even, ring, own))
    ring = arrival(ring)
    other = arrival(other)
    base = 0
    for c, (spot, _, _, size) in enumerate(layouts):
        put_ring(place_ref, keep, send, spot, base, c, row_dot(ring[c * UNIT : (c + 1) * UNIT], own))
        base += size
    for a in range(units):
        block = row_dot(chosen[a * UNIT : (a + 1) * UNIT], other)
        for b in range(units):
            step = max(a, b)
            base = sum(layouts[s][3] for s in range(step))
            put_third(place_ref, keep, send, layouts[step][0], base, a, b, lanes(block, b))


PARTS = 1


def own_copies(own_hbm, own, sems):
    deep = own.shape[0] // PARTS
    spans = [pl.ds(k * deep, deep) for k in range(PARTS)]
    return [pltpu.make_async_copy(own_hbm.at[at], own.at[at], sems.at[i]) for i, at in enumerate(spans)]


def grads_kernel(step, spot, place_ref, own_hbm, *refs):
    n = step + 1
    mine, ring, other, (keep, send, own, fresh, chosen, others, sems) = refs[:n], refs[n : 2 * n], refs[2 * n : 3 * n], refs[3 * n :]
    even = place_ref[0] == 0
    deep = own.shape[0] // PARTS

    def column(ref, a):
        return ref.at[:, a * UNIT : (a + 1) * UNIT]

    first = pltpu.make_async_copy(ring[step], fresh, sems.at[PARTS])
    copies = own_copies(own_hbm, own, sems)
    third = [pltpu.make_async_copy(other[a], column(others, a), sems.at[PARTS + 1 + a]) for a in range(n)]
    from_ring = [pltpu.make_async_copy(ring[a], column(chosen, a), sems.at[PARTS + 1 + n + a]) for a in range(n)]
    from_mine = [pltpu.make_async_copy(mine[a], column(chosen, a), sems.at[PARTS + 1 + n + a]) for a in range(n)]
    first.start()
    for copy in copies:
        copy.start()

    @pl.when(even)
    def _():
        for copy in from_ring:
            copy.start()

    @pl.when(jnp.logical_not(even))
    def _():
        for copy in from_mine:
            copy.start()

    for copy in third:
        copy.start()
    first.wait()
    block = jnp.zeros((UNIT, own.shape[1]), jnp.float32)
    for copy, k in zip(copies, range(PARTS)):
        copy.wait()
        at = pl.ds(k * deep, deep)
        block = block + dot(fresh[at, :].T, own[at, :], ((1,), (0,)))
    put_ring(place_ref, keep, send, spot, 0, step, block)
    for copy in from_ring + third:
        copy.wait()
    block = dot(column(chosen, step)[...].T, others[...], ((1,), (0,)))
    for b in range(n):
        put_third(place_ref, keep, send, spot, 0, step, b, lanes(block, b))
    if step:
        block = dot(column(others, step)[...].T, chosen[:, : step * UNIT], ((1,), (0,))).T
        for a in range(step):
            put_third(place_ref, keep, send, spot, 0, a, step, block[a * UNIT : (a + 1) * UNIT])


def grads_scratch(own, n):
    deep = own.shape[0]
    arrays = [pltpu.VMEM((deep, width), jnp.bfloat16) for width in (own.shape[1], UNIT, n * UNIT, n * UNIT)]
    return (*arrays, pltpu.SemaphoreType.DMA((PARTS + 1 + 2 * n,)))


def product(acts, grads, act_at, grad_at, rows):
    act_sum = acts[0][act_at : act_at + rows, :] + acts[1][act_at : act_at + rows, :]
    grad_sum = grads[0][grad_at : grad_at + rows, :] + grads[1][grad_at : grad_at + rows, :]
    return (act_sum * (1.0 / math.sqrt(D))) * (grad_sum * (1.0 / math.sqrt(FF)))


def return_kernel(layouts, steps, *refs):
    acts, (ring, swap) = refs[:2], refs[-2:]
    ring_at = swap_at = 0
    for i, c in enumerate(steps):
        grads = refs[2 + 2 * i : 4 + 2 * i]
        _, n_ring, n_swap, _ = layouts[c]
        base = sum(layouts[s][3] for s in range(c))
        ring[ring_at : ring_at + n_ring, :] = product(acts, grads, base, 0, n_ring)
        swap[swap_at : swap_at + n_swap - n_ring, :] = product(acts, grads, base + n_ring, n_ring, n_swap - n_ring)
        ring_at += n_ring
        swap_at += n_swap - n_ring


def last_kernel(base, first, *refs):
    acts, near, far, out = refs[:2], refs[2], refs[3], refs[4]
    n = out.shape[0]
    near_part = near.at[first : first + n, :]
    out[...] = product(acts, (near_part, far), base + first, 0, n)


def final_kernel(layouts, groups, place_ref, lengths_ref, *refs):
    units = len(layouts)
    last = units - 1
    selves, acts, out = refs[:2], refs[2:4], refs[-1]
    grads = [refs[4 + 2 * c : 6 + 2 * c] for c in range(last)]
    near, far_ring, far_rest = refs[4 + 2 * last : 7 + 2 * last]
    rings, swaps = refs[7 + 2 * last : -1 : 2], refs[8 + 2 * last : -1 : 2]
    returned = {last: (rings[-1], 0, swaps[-1], -layouts[last][1])}
    for i, steps in enumerate(groups):
        ring_at = swap_at = 0
        for c in steps:
            _, n_ring, n_swap, _ = layouts[c]
            returned[c] = rings[i], ring_at, swaps[i], swap_at - n_ring
            ring_at += n_ring
            swap_at += n_swap - n_ring
    even = place_ref[0] == 0
    width = place_ref[3]
    token = place_ref[4]
    total = lengths_ref.shape[0]
    here = lengths_ref[token]
    columns = width * UNIT + lax.broadcasted_iota(jnp.int32, (UNIT, UNIT), 1)
    line = lax.broadcasted_iota(jnp.int32, (UNIT, UNIT), 0)

    def block(where, name, step):
        spot = layouts[step][0][name]
        size = UNIT if name[0] == "rt" else SUB
        if where == "local":
            base = sum(layouts[s][3] for s in range(step))
            if step < last:
                return product(acts, grads[step], base + spot, spot, size)
            _, n_ring, n_swap, _ = layouts[last]
            far, at = (far_ring, spot) if spot < n_ring else (far_rest, spot - n_swap)
            return product(acts, (near.at[spot : spot + size, :], far.at[at : at + size, :]), base + spot, 0, size)
        ring, ring_at, swap, swap_at = returned[step]
        ref, at = (ring, ring_at + spot) if where == "ring" else (swap, swap_at + spot)
        return ref[at : at + size, :]

    def natural(offset, b, tile, there):
        live = (b * UNIT + line < here) & (columns < there)
        out[offset, b * UNIT : (b + 1) * UNIT, :] = jnp.where(live, tile.T, 0.0)

    def arrival(offset, c, tile, there):
        token_at = (line // SUB) * UNIT + c * SUB + line % SUB
        tile = jnp.where((token_at < here) & (columns < there), tile.T, 0.0)
        for q in range(WID):
            first = q * UNIT + c * SUB
            out[offset, first : first + SUB, :] = tile[q * SUB : (q + 1) * SUB]

    there = [lengths_ref[lax.rem(token + offset + total - 2, total)] for offset in range(5)]
    for c in range(units):
        arrival(0, c, block("ring", ("rt", c), c), there[0])
        tt = [jnp.concatenate([block(r, ("tt", a, c), max(a, c)) for a in range(units)], axis=0) for r in ("ring", "local")]
        arrival(1, c, jnp.where(even, tt[0], tt[1]), there[1])
        arrival(3, c, jnp.concatenate([block("swap", ("tj", a, c), max(a, c)) for a in range(units)], axis=0), there[3])
    for b in range(WID):
        natural(2, b, product(selves, selves, b * UNIT, (WID + b) * UNIT, UNIT), there[2])
        natural(4, b, jnp.concatenate([block("local", ("rj", c, b), c) for c in range(units)], axis=0), there[4])


def shards(acts, grads, lengths):
    rows = acts.shape[0]
    units = rows // UNIT
    length = lax.axis_size("tok")
    token = lax.axis_index("tok")
    width = lax.axis_index("wid")
    place = jnp.stack([token % 2, width % 2, width // 2, width, token]).astype(jnp.int32)
    swap = [(i, i ^ 1) for i in range(length)]
    down = [(i, (i - 2) % length) for i in range(length)]
    up = [(i, (i + 2) % length) for i in range(length)]
    layouts = [step_layout(c, units) for c in range(units)]

    def floats(n):
        return (jax.ShapeDtypeStruct((2, n, UNIT), jnp.float32),) * 2

    def over_core(send):
        return lax.ppermute(send, "wid", [(w, w ^ 1) for w in range(WID)])

    own_g = grads.T
    mine = list(call(reorder_kernel, (jax.ShapeDtypeStruct((grads.shape[1], UNIT), jnp.bfloat16),) * units, own_g))
    alive = jnp.max(lengths) > 0
    seen = {}

    def after(x, names):
        if not names:
            return x
        x, *held = lax.optimization_barrier((x, *[seen[name] for name in names]))
        seen.update(zip(names, held))
        return x

    def start(name, chunk):
        seen["R" + name] = lax.ppermute(after(chunk, GATES.get("R" + name)), "tok", down)
        seen["O" + name] = lax.ppermute(after(chunk, GATES.get("O" + name)), "tok", swap)

    def exchange(name, kernel, n, first, *rest, cuts=(), **options):
        spans = list(zip((0, *cuts), (*cuts, n)))

        def summed(*args):
            keep, send = call(kernel, floats(n), place, *args, scalars=1, **options)
            arrived = over_core(send)
            return keep[0] + arrived[0], *[keep[1, a:b] + arrived[1, a:b] for a, b in spans]

        def nothing(*args):
            return tuple(jnp.zeros((b - a, UNIT), jnp.float32) for a, b in [(0, n)] + spans)

        first = after(first, GATES.get("K" + name))
        run = summed if name in PLAIN else lambda *args: lax.cond(alive, summed, nothing, *args)
        near, *far = run(first, *rest)
        for i, x in enumerate(far):
            label = "S" + name + "xyz"[i : i + 1] * (len(far) > 1)
            seen[label] = lax.ppermute(after(x, GATES.get(label)), "wid", [(w, w ^ 2) for w in range(WID)])
        return near

    def pair(c):
        if str(c) in PIECES:
            return seen["R%d" % c], seen["O%d" % c]
        return tuple(jnp.concatenate([seen["%s%d%s" % (side, c, half)] for half in "ab"], axis=0) for side in "RO")

    near = {}

    def send_back(i, steps):
        sizes = [sum(layouts[c][1] for c in steps), sum(layouts[c][2] - layouts[c][1] for c in steps)]
        first = after(near[steps[0]], GATES.get("G%d" % i))
        grams = sum([[first if c == steps[0] else near[c], seen["S%d" % c]] for c in steps], [])
        ring, swapped = call(
            lambda *refs: return_kernel(layouts, steps, *refs),
            tuple(jax.ShapeDtypeStruct((n, UNIT), jnp.float32) for n in sizes),
            near["A"], seen["SA"], *grams,
        )
        seen["V%d" % i] = ring
        seen["U%d" % i] = lax.ppermute(ring, "tok", up)
        seen["X%d" % i] = lax.ppermute(swapped, "tok", swap)

    for piece in PIECES:
        if piece == "A":
            start(piece, acts)
        elif piece[0] in "0123":
            chunk = mine[int(piece[0])]
            cut = chunk.shape[0] // 2
            start(piece, {"": chunk, "a": chunk[:cut], "b": chunk[cut:]}[piece[1:]])
        elif piece[0] == "g":
            send_back(int(piece[1:]), GROUPS[int(piece[1:])])
        elif piece == "kS":
            near["S"] = exchange("S", self_kernel, 2 * WID * UNIT, acts, own_g)
        elif piece == "kA":
            everything = sum(size for _, _, _, size in layouts)
            near["A"] = exchange("A", lambda *refs: acts_kernel(layouts, *refs), everything, acts, seen["RA"], seen["OA"])
        else:
            c = int(piece[1])
            spot, size = layouts[c][0], layouts[c][3]
            pairs = [pair(a) for a in range(c + 1)]
            near[c] = seen["N%d" % c] = exchange(
                piece[1], lambda *refs, c=c, spot=spot: grads_kernel(c, spot, *refs),
                size, own_g, *mine[: c + 1], *[p[0] for p in pairs], *[p[1] for p in pairs],
                memory=pl.BlockSpec(memory_space=pl.ANY), scratch=grads_scratch(own_g, c + 1),
                cuts=layouts[c][1:3] if c + 1 == units else (),
            )

    returned = []
    for i in range(len(GROUPS)):
        returned += [seen["U%d" % i], seen["X%d" % i]]

    last = units - 1
    base = sum(layout[3] for layout in layouts[:last])
    _, n_ring, n_swap, _ = layouts[last]
    for first, n, far, move in ((0, n_ring, "S%dx" % last, up), (n_ring, n_swap - n_ring, "S%dy" % last, swap)):
        tile = call(
            lambda *refs, first=first: last_kernel(base, first, *refs),
            jax.ShapeDtypeStruct((n, UNIT), jnp.float32), near["A"], seen["SA"], near[last], seen[far],
        )
        returned.append(lax.ppermute(tile, "tok", move))

    grams = sum([[near[c], seen["S%d" % c]] for c in range(last)], [near["A"], seen["SA"]])
    grams += [near[last], seen["S%dx" % last], seen["S%dz" % last]]
    out = call(
        lambda *refs: final_kernel(layouts, GROUPS, *refs),
        jax.ShapeDtypeStruct((5, rows, UNIT), jnp.float32),
        place, lengths, near["S"], seen["SS"], *grams, *returned, scalars=2,
    )
    return out.transpose(1, 0, 2)


def solution(mesh):
    return jax.shard_map(
        shards,
        mesh=mesh,
        in_specs=(P("tok", "wid"), P("tok", "wid"), P()),
        out_specs=P("tok", None, "wid"),
        check_vma=False,
    )
```

```python
import math

import jax
import jax.numpy as jnp
from jax import lax
from jax.experimental import pallas as pl
from jax.experimental.pallas import tpu as pltpu
from jax.sharding import PartitionSpec as P

D = 4096
FF = 11008
WID = 4
UNIT = 128
SUB = UNIT // WID
VMEM_LIMIT = 24 << 20
PIECES = ['A', '0', 'kS', '1', 'kA', '2', 'k0', '3', 'k1', 'g0', 'k2', 'g1', 'k3']
GATES = {'R1': ['RA'], 'O1': ['OA'], 'R2': ['RA'], 'O2': ['OA'], 'R3': ['R0'], 'O3': ['O0'], 'KA': [], 'K0': ['SS'], 'K1': ['SS'], 'K2': ['S0'], 'K3': ['V0'], 'SA': [], 'S0': [], 'S1': ['S0'], 'S2': ['S1'], 'S3x': [], 'S3y': [], 'S3z': ['S3x'], 'G0': [], 'G1': []}
PLAIN = []
GROUPS = [[0, 1], [2]]
SMEM = pl.BlockSpec(memory_space=pltpu.SMEM)
VMEM = pl.BlockSpec(memory_space=pltpu.VMEM)


def call(kernel, outs, *args, scalars=0, memory=VMEM, scratch=()):
    return pl.pallas_call(
        kernel,
        out_shape=outs,
        in_specs=[SMEM] * scalars + [memory] * (len(args) - scalars),
        out_specs=jax.tree.map(lambda _: VMEM, outs),
        scratch_shapes=scratch,
        cost_estimate=pl.CostEstimate(flops=2000000000, bytes_accessed=2000000, transcendentals=0),
        compiler_params=pltpu.CompilerParams(vmem_limit_bytes=VMEM_LIMIT),
    )(*args)


def dot(left, right, dims):
    return lax.dot_general(left, right, (dims, ((), ())), preferred_element_type=jnp.float32)


def row_dot(left, right):
    return dot(left, right, ((1,), (1,)))


def put(place_ref, keep, send, at, quarters):
    core = place_ref[1] == 0
    side = place_ref[2] == 0
    rows = pl.ds(at, quarters[0].shape[0])
    kept = [jnp.where(core, quarters[2 * s], quarters[2 * s + 1]) for s in range(2)]
    sent = [jnp.where(core, quarters[2 * s + 1], quarters[2 * s]) for s in range(2)]
    for ref, pair in ((keep, kept), (send, sent)):
        ref[0, rows, :] = jnp.where(side, pair[0], pair[1])
        ref[1, rows, :] = jnp.where(side, pair[1], pair[0])


def split_rows(block):
    n = block.shape[0] // WID
    return [block[q * n : (q + 1) * n] for q in range(WID)]


def lanes(block, b):
    return block[:, b * UNIT : (b + 1) * UNIT]


def step_layout(step, units):
    fresh = [(step, b) for b in range(step + 1)] + [(a, step) for a in range(step)]
    at, spot = UNIT, {("rt", step): 0}
    for a, b in fresh:
        spot[("tt", b, a)] = at
        at += SUB
    n_ring = at
    for a, b in fresh:
        spot[("tj", a, b)] = at
        at += SUB
    n_swap = at
    for b in range(WID):
        spot[("rj", step, b)] = at
        at += SUB
    return spot, n_ring, n_swap, at


def put_ring(place_ref, keep, send, spot, base, step, block):
    columns = [lanes(block, b) for b in range(WID)]
    put(place_ref, keep, send, base + spot[("rt", step)], [c.T for c in columns])
    for b in range(WID):
        put(place_ref, keep, send, base + spot[("rj", step, b)], split_rows(columns[b]))


def put_third(place_ref, keep, send, spot, base, a, b, block):
    put(place_ref, keep, send, base + spot[("tj", a, b)], split_rows(block))
    put(place_ref, keep, send, base + spot[("tt", b, a)], split_rows(block.T))


def reorder_kernel(g_ref, *outs):
    units = len(outs)
    tokens = g_ref.shape[1]
    source = lax.broadcasted_iota(jnp.int32, (tokens, UNIT), 0)
    lane = lax.broadcasted_iota(jnp.int32, (tokens, UNIT), 1)
    for c, out in enumerate(outs):
        wanted = (lane // SUB) * UNIT + c * SUB + lane % SUB
        pick = jnp.where(source == wanted, 1.0, 0.0).astype(jnp.bfloat16)
        out[...] = dot(g_ref[...], pick, ((1,), (0,))).astype(jnp.bfloat16)


def self_kernel(place_ref, a_ref, g_ref, keep, send):
    acts = a_ref[...]
    grads = g_ref[...]
    for i, block in enumerate((row_dot(acts, acts), dot(grads.T, grads, ((1,), (0,))))):
        for b in range(WID):
            put(place_ref, keep, send, (i * WID + b) * UNIT, split_rows(lanes(block, b)))


def acts_kernel(layouts, place_ref, own_ref, ring_ref, other_ref, keep, send):
    units = len(layouts)
    even = place_ref[0] == 0

    def arrival(x):
        return jnp.concatenate([x[q * UNIT + c * SUB : q * UNIT + (c + 1) * SUB] for c in range(units) for q in range(WID)], axis=0)

    own, ring, other = own_ref[...], ring_ref[...], other_ref[...]
    chosen = arrival(jnp.where(even, ring, own))
    ring = arrival(ring)
    other = arrival(other)
    base = 0
    for c, (spot, _, _, size) in enumerate(layouts):
        put_ring(place_ref, keep, send, spot, base, c, row_dot(ring[c * UNIT : (c + 1) * UNIT], own))
        base += size
    for a in range(units):
        block = row_dot(chosen[a * UNIT : (a + 1) * UNIT], other)
        for b in range(units):
            step = max(a, b)
            base = sum(layouts[s][3] for s in range(step))
            put_third(place_ref, keep, send, layouts[step][0], base, a, b, lanes(block, b))


PARTS = 1


def own_copies(own_hbm, own, sems):
    deep = own.shape[0] // PARTS
    spans = [pl.ds(k * deep, deep) for k in range(PARTS)]
    return [pltpu.make_async_copy(own_hbm.at[at], own.at[at], sems.at[i]) for i, at in enumerate(spans)]


def grads_kernel(step, spot, place_ref, own_hbm, *refs):
    n = step + 1
    mine, ring, other, (keep, send, own, fresh, chosen, others, sems) = refs[:n], refs[n : 2 * n], refs[2 * n : 3 * n], refs[3 * n :]
    even = place_ref[0] == 0
    deep = own.shape[0] // PARTS

    def column(ref, a):
        return ref.at[:, a * UNIT : (a + 1) * UNIT]

    first = pltpu.make_async_copy(ring[step], fresh, sems.at[PARTS])
    copies = own_copies(own_hbm, own, sems)
    third = [pltpu.make_async_copy(other[a], column(others, a), sems.at[PARTS + 1 + a]) for a in range(n)]
    from_ring = [pltpu.make_async_copy(ring[a], column(chosen, a), sems.at[PARTS + 1 + n + a]) for a in range(step)]
    from_mine = [pltpu.make_async_copy(mine[a], column(chosen, a), sems.at[PARTS + 1 + n + a]) for a in range(n)]
    first.start()
    for copy in copies:
        copy.start()

    @pl.when(even)
    def _():
        for copy in from_ring[:step]:
            copy.start()

    @pl.when(jnp.logical_not(even))
    def _():
        for copy in from_mine:
            copy.start()

    for copy in third:
        copy.start()
    first.wait()
    block = jnp.zeros((UNIT, own.shape[1]), jnp.float32)
    for copy, k in zip(copies, range(PARTS)):
        copy.wait()
        at = pl.ds(k * deep, deep)
        block = block + dot(fresh[at, :].T, own[at, :], ((1,), (0,)))
    put_ring(place_ref, keep, send, spot, 0, step, block)
    for copy in from_ring[:step] + third:
        copy.wait()

    @pl.when(jnp.logical_not(even))
    def _():
        from_mine[step].wait()

    newest = jnp.where(even, fresh[...], column(chosen, step)[...])
    block = dot(newest.T, others[...], ((1,), (0,)))
    for b in range(n):
        put_third(place_ref, keep, send, spot, 0, step, b, lanes(block, b))
    if step:
        block = dot(column(others, step)[...].T, chosen[:, : step * UNIT], ((1,), (0,))).T
        for a in range(step):
            put_third(place_ref, keep, send, spot, 0, a, step, block[a * UNIT : (a + 1) * UNIT])


def grads_scratch(own, n):
    deep = own.shape[0]
    arrays = [pltpu.VMEM((deep, width), jnp.bfloat16) for width in (own.shape[1], UNIT, n * UNIT, n * UNIT)]
    return (*arrays, pltpu.SemaphoreType.DMA((PARTS + 1 + 2 * n,)))


def product(acts, grads, act_at, grad_at, rows):
    act_sum = acts[0][act_at : act_at + rows, :] + acts[1][act_at : act_at + rows, :]
    grad_sum = grads[0][grad_at : grad_at + rows, :] + grads[1][grad_at : grad_at + rows, :]
    return (act_sum * (1.0 / math.sqrt(D))) * (grad_sum * (1.0 / math.sqrt(FF)))


def return_kernel(layouts, steps, *refs):
    acts, (ring, swap) = refs[:2], refs[-2:]
    ring_at = swap_at = 0
    for i, c in enumerate(steps):
        grads = refs[2 + 2 * i : 4 + 2 * i]
        _, n_ring, n_swap, _ = layouts[c]
        base = sum(layouts[s][3] for s in range(c))
        ring[ring_at : ring_at + n_ring, :] = product(acts, grads, base, 0, n_ring)
        swap[swap_at : swap_at + n_swap - n_ring, :] = product(acts, grads, base + n_ring, n_ring, n_swap - n_ring)
        ring_at += n_ring
        swap_at += n_swap - n_ring


def last_kernel(base, first, *refs):
    acts, near, far, out = refs[:2], refs[2], refs[3], refs[4]
    n = out.shape[0]
    near_part = near.at[first : first + n, :]
    out[...] = product(acts, (near_part, far), base + first, 0, n)


def final_kernel(layouts, groups, place_ref, lengths_ref, *refs):
    units = len(layouts)
    last = units - 1
    selves, acts, out = refs[:2], refs[2:4], refs[-1]
    grads = [refs[4 + 2 * c : 6 + 2 * c] for c in range(last)]
    near, far_ring, far_rest = refs[4 + 2 * last : 7 + 2 * last]
    rings, swaps = refs[7 + 2 * last : -1 : 2], refs[8 + 2 * last : -1 : 2]
    returned = {last: (rings[-1], 0, swaps[-1], -layouts[last][1])}
    for i, steps in enumerate(groups):
        ring_at = swap_at = 0
        for c in steps:
            _, n_ring, n_swap, _ = layouts[c]
            returned[c] = rings[i], ring_at, swaps[i], swap_at - n_ring
            ring_at += n_ring
            swap_at += n_swap - n_ring
    even = place_ref[0] == 0
    width = place_ref[3]
    token = place_ref[4]
    total = lengths_ref.shape[0]
    here = lengths_ref[token]
    columns = width * UNIT + lax.broadcasted_iota(jnp.int32, (UNIT, UNIT), 1)
    line = lax.broadcasted_iota(jnp.int32, (UNIT, UNIT), 0)

    def block(where, name, step):
        spot = layouts[step][0][name]
        size = UNIT if name[0] == "rt" else SUB
        if where == "local":
            base = sum(layouts[s][3] for s in range(step))
            if step < last:
                return product(acts, grads[step], base + spot, spot, size)
            _, n_ring, n_swap, _ = layouts[last]
            far, at = (far_ring, spot) if spot < n_ring else (far_rest, spot - n_swap)
            return product(acts, (near.at[spot : spot + size, :], far.at[at : at + size, :]), base + spot, 0, size)
        ring, ring_at, swap, swap_at = returned[step]
        ref, at = (ring, ring_at + spot) if where == "ring" else (swap, swap_at + spot)
        return ref[at : at + size, :]

    def natural(offset, b, tile, there):
        live = (b * UNIT + line < here) & (columns < there)
        out[offset, b * UNIT : (b + 1) * UNIT, :] = jnp.where(live, tile.T, 0.0)

    def arrival(offset, c, tile, there):
        token_at = (line // SUB) * UNIT + c * SUB + line % SUB
        tile = jnp.where((token_at < here) & (columns < there), tile.T, 0.0)
        for q in range(WID):
            first = q * UNIT + c * SUB
            out[offset, first : first + SUB, :] = tile[q * SUB : (q + 1) * SUB]

    there = [lengths_ref[lax.rem(token + offset + total - 2, total)] for offset in range(5)]
    for c in range(units):
        arrival(0, c, block("ring", ("rt", c), c), there[0])
        tt = [jnp.concatenate([block(r, ("tt", a, c), max(a, c)) for a in range(units)], axis=0) for r in ("ring", "local")]
        arrival(1, c, jnp.where(even, tt[0], tt[1]), there[1])
        arrival(3, c, jnp.concatenate([block("swap", ("tj", a, c), max(a, c)) for a in range(units)], axis=0), there[3])
    for b in range(WID):
        natural(2, b, product(selves, selves, b * UNIT, (WID + b) * UNIT, UNIT), there[2])
        natural(4, b, jnp.concatenate([block("local", ("rj", c, b), c) for c in range(units)], axis=0), there[4])


def shards(acts, grads, lengths):
    rows = acts.shape[0]
    units = rows // UNIT
    length = lax.axis_size("tok")
    token = lax.axis_index("tok")
    width = lax.axis_index("wid")
    place = jnp.stack([token % 2, width % 2, width // 2, width, token]).astype(jnp.int32)
    swap = [(i, i ^ 1) for i in range(length)]
    down = [(i, (i - 2) % length) for i in range(length)]
    up = [(i, (i + 2) % length) for i in range(length)]
    layouts = [step_layout(c, units) for c in range(units)]

    def floats(n):
        return (jax.ShapeDtypeStruct((2, n, UNIT), jnp.float32),) * 2

    def over_core(send):
        return lax.ppermute(send, "wid", [(w, w ^ 1) for w in range(WID)])

    own_g = grads.T
    mine = list(call(reorder_kernel, (jax.ShapeDtypeStruct((grads.shape[1], UNIT), jnp.bfloat16),) * units, own_g))
    alive = jnp.max(lengths) > 0
    seen = {}

    def after(x, names):
        if not names:
            return x
        x, *held = lax.optimization_barrier((x, *[seen[name] for name in names]))
        seen.update(zip(names, held))
        return x

    def start(name, chunk):
        seen["R" + name] = lax.ppermute(after(chunk, GATES.get("R" + name)), "tok", down)
        seen["O" + name] = lax.ppermute(after(chunk, GATES.get("O" + name)), "tok", swap)

    def exchange(name, kernel, n, first, *rest, cuts=(), **options):
        spans = list(zip((0, *cuts), (*cuts, n)))

        def summed(*args):
            keep, send = call(kernel, floats(n), place, *args, scalars=1, **options)
            arrived = over_core(send)
            return keep[0] + arrived[0], *[keep[1, a:b] + arrived[1, a:b] for a, b in spans]

        def nothing(*args):
            return tuple(jnp.zeros((b - a, UNIT), jnp.float32) for a, b in [(0, n)] + spans)

        first = after(first, GATES.get("K" + name))
        run = summed if name in PLAIN else lambda *args: lax.cond(alive, summed, nothing, *args)
        near, *far = run(first, *rest)
        for i, x in enumerate(far):
            label = "S" + name + "xyz"[i : i + 1] * (len(far) > 1)
            seen[label] = lax.ppermute(after(x, GATES.get(label)), "wid", [(w, w ^ 2) for w in range(WID)])
        return near

    def pair(c):
        if str(c) in PIECES:
            return seen["R%d" % c], seen["O%d" % c]
        return tuple(jnp.concatenate([seen["%s%d%s" % (side, c, half)] for half in "ab"], axis=0) for side in "RO")

    near = {}

    def send_back(i, steps):
        sizes = [sum(layouts[c][1] for c in steps), sum(layouts[c][2] - layouts[c][1] for c in steps)]
        first = after(near[steps[0]], GATES.get("G%d" % i))
        grams = sum([[first if c == steps[0] else near[c], seen["S%d" % c]] for c in steps], [])
        ring, swapped = call(
            lambda *refs: return_kernel(layouts, steps, *refs),
            tuple(jax.ShapeDtypeStruct((n, UNIT), jnp.float32) for n in sizes),
            near["A"], seen["SA"], *grams,
        )
        seen["V%d" % i] = ring
        seen["U%d" % i] = lax.ppermute(ring, "tok", up)
        seen["X%d" % i] = lax.ppermute(swapped, "tok", swap)

    for piece in PIECES:
        if piece == "A":
            start(piece, acts)
        elif piece[0] in "0123":
            chunk = mine[int(piece[0])]
            cut = chunk.shape[0] // 2
            start(piece, {"": chunk, "a": chunk[:cut], "b": chunk[cut:]}[piece[1:]])
        elif piece[0] == "g":
            send_back(int(piece[1:]), GROUPS[int(piece[1:])])
        elif piece == "kS":
            near["S"] = exchange("S", self_kernel, 2 * WID * UNIT, acts, own_g)
        elif piece == "kA":
            everything = sum(size for _, _, _, size in layouts)
            near["A"] = exchange("A", lambda *refs: acts_kernel(layouts, *refs), everything, acts, seen["RA"], seen["OA"])
        else:
            c = int(piece[1])
            spot, size = layouts[c][0], layouts[c][3]
            pairs = [pair(a) for a in range(c + 1)]
            near[c] = seen["N%d" % c] = exchange(
                piece[1], lambda *refs, c=c, spot=spot: grads_kernel(c, spot, *refs),
                size, own_g, *mine[: c + 1], *[p[0] for p in pairs], *[p[1] for p in pairs],
                memory=pl.BlockSpec(memory_space=pl.ANY), scratch=grads_scratch(own_g, c + 1),
                cuts=layouts[c][1:3] if c + 1 == units else (),
            )

    returned = []
    for i in range(len(GROUPS)):
        returned += [seen["U%d" % i], seen["X%d" % i]]

    last = units - 1
    base = sum(layout[3] for layout in layouts[:last])
    _, n_ring, n_swap, _ = layouts[last]
    for first, n, far, move in ((0, n_ring, "S%dx" % last, up), (n_ring, n_swap - n_ring, "S%dy" % last, swap)):
        tile = call(
            lambda *refs, first=first: last_kernel(base, first, *refs),
            jax.ShapeDtypeStruct((n, UNIT), jnp.float32), near["A"], seen["SA"], near[last], seen[far],
        )
        returned.append(lax.ppermute(tile, "tok", move))

    grams = sum([[near[c], seen["S%d" % c]] for c in range(last)], [near["A"], seen["SA"]])
    grams += [near[last], seen["S%dx" % last], seen["S%dz" % last]]
    out = call(
        lambda *refs: final_kernel(layouts, GROUPS, *refs),
        jax.ShapeDtypeStruct((5, rows, UNIT), jnp.float32),
        place, lengths, near["S"], seen["SS"], *grams, *returned, scalars=2,
    )
    return out.transpose(1, 0, 2)


def solution(mesh):
    return jax.shard_map(
        shards,
        mesh=mesh,
        in_specs=(P("tok", "wid"), P("tok", "wid"), P()),
        out_specs=P("tok", None, "wid"),
        check_vma=False,
    )
```
